32 devices in a mesh: group: 2 (over x), expert: 4 (over y, core), tensor: 4 (over z).
Axes of the slice: x: 2, y: 2, z: 4, core: 2. Of those that a mesh axis runs over, the one named last changes fastest.
Arguments:
- x_tokens: bfloat16 [256, 3072], P(('group', 'expert', 'tensor')), parts along dimension 0, may hold values from -6 to 6
- grad_values: bfloat16 [256, 3072], P(('group', 'expert', 'tensor')), parts along dimension 0, may hold values from -6 to 6
- grad_scale: float32 [256], P(('group', 'expert', 'tensor')), parts along dimension 0, may hold values from 0.05 to 1
- combine: float32 [256, 2], P(('group', 'expert', 'tensor')), parts along dimension 0, may hold values from 0.1 to 0.9
- routes: int32 [256, 2], P(('group', 'expert', 'tensor')), parts along dimension 0, may hold values from 0 to 3, all different within a row; in each aligned block of 8 rows (0 to 7, 8 to 15, ...) at most 5 rows name the same one
- pattern: int32 [4, 768], replicated, may hold values from 0 to 5
- w_gate: bfloat16 [1536, 32768], P(None, ('expert', 'tensor')), may hold values from -0.15625 to 0.15625
- w_up: bfloat16 [1536, 32768], P(None, ('expert', 'tensor')), may hold values from -0.15625 to 0.15625
- w_down: bfloat16 [32768, 1536], P(('expert', 'tensor')), may hold values from -0.0625 to 0.0625
Outputs:
- grad_tokens: bfloat16 [256, 3072], P(('group', 'expert', 'tensor')), parts along dimension 0
- grad_gate: bfloat16 [3072, 32768], P('group', ('expert', 'tensor')), parts along dimension 0
- grad_up: bfloat16 [3072, 32768], P('group', ('expert', 'tensor')), parts along dimension 0
- grad_down: bfloat16 [32768, 3072], P(('expert', 'tensor'), 'group'), parts along dimension 1
The draws below stay inside these ranges and needn't reach their ends.
There are 2 independent parts, one for each index of `group`. The reference program is written for one: setup_inputs(seed, part) draws one part's arguments, and reference() takes and returns one part's arrays. A program takes and returns all parts, laid end to end along the dimension named above; an argument that names none is the same for every part. Nothing has to cross between parts.
Inputs may be any that keep to these rules, and one draw needn't show every extreme that they name: `routes`: in the rows of one device (8 aligned rows), no expert is named by more than 5 rows, and some device's rows name one expert exactly 5 times; a token's two experts differ.
All inputs are finite; a program needn't handle non-finite values.
Results may differ from the reference program's by a relative error of at most 0.0058.
Values may be sent and summed in bfloat16 or wider, within the bound.
No kernel may reach another device: no remote copies, remote signals or barrier semaphores. Data moves between devices by JAX's collectives and lax.ppermute only.
A program may use at most 128 MiB of HBM per device.

```python
import math
import jax
import jax.numpy as jnp
import numpy as np

D = 3072
FF = 8192
EXPERTS = 4
TOK_DEV = 8
MOST = 5
KEPT = 1536
GROUPS = 768
TOKENS = 128


def plant(values, rng, smallest, high):
    extent = values.shape
    spot = [jax.random.randint(jax.random.fold_in(rng, axis), (), 0, extent[axis]) for axis in range(len(extent))]
    values = values.at[tuple(spot)].set(smallest)
    longest = extent.index(max(extent))
    spot[longest] = (spot[longest] + 1) % extent[longest]
    return values.at[tuple(spot)].set(high)


def block_scale(stream_key, extent, split, smallest, top_value):
    gain, own = 1.0, jax.random.fold_in(stream_key, 6)
    for axis_at, parts in split:
        heights = jnp.exp(jax.random.uniform(jax.random.fold_in(own, axis_at), (parts,), jnp.float32, smallest / len(split), top_value / len(split)))
        gain = gain * jnp.repeat(heights, extent[axis_at] // parts).reshape([-1 if axis == axis_at else 1 for axis in range(len(extent))])
    return gain


def routed_block(stream_key, own, number, rows, amount, top, reach, lean):
    sequence = jax.random.permutation(stream_key, amount)
    packed, common = load_shares(amount, rows * top, reach, lean, True), load_shares(amount, rows * top, reach, lean, False)
    places = jnp.arange(amount)

    def named(lengths, offset_by):
        used = int((lengths > 0).sum())
        fixed = max(1, used // 4)
        shifted = fixed + (places - fixed + offset_by * (used - fixed)) % max(1, amount - fixed)
        return jnp.zeros((amount,), jnp.int32).at[sequence[jnp.where(places < fixed, places, shifted)]].set(jnp.asarray(lengths, jnp.int32))

    lengths = jnp.where(number % 4 == 0, named(packed, number // 4), named(common, number - number // 4 - 1))
    mixed = jax.random.permutation(jax.random.fold_in(own, 3), amount)
    source_of, taker = mixed[0:amount // 2 * 2:2], mixed[1:amount // 2 * 2:2]
    slack = jnp.minimum(lengths[source_of] - 1, reach - lengths[taker]) // 2
    slack = jnp.where((source_of == sequence[0]) | (taker == sequence[0]) | (lengths[taker] == 0), 0, jnp.maximum(slack, 0))
    shifted = jax.random.randint(jax.random.fold_in(own, 4), (amount // 2,), 0, 1 << 20) % (slack + 1)
    lengths = lengths.at[source_of].add(-shifted).at[taker].add(shifted)
    items = jnp.searchsorted(jnp.cumsum(lengths), jnp.arange(rows * top), side="right").astype(jnp.int32)
    grid = items.reshape(top, rows).T
    grid = grid[jax.random.permutation(jax.random.fold_in(own, 1), rows)]
    offset_by = jax.random.randint(jax.random.fold_in(own, 2), (rows, 1), 0, top)
    return jnp.take_along_axis(grid, (jnp.arange(top)[None, :] + offset_by) % top, axis=1)


def load_shares(count, total, most, slope, full):
    portions = [(1 << 20) // math.isqrt(rank ** slope) + 1 for rank in range(1, count + 1)]
    largest = most if full else min(most, max(-(-total // count), total * portions[0] // sum(portions)))
    least = 1 if total - largest >= count - 1 else 0
    counts, rest = [largest] + [least] * (count - 1), total - largest - least * (count - 1)
    while rest > 0:
        candidates = [i for i in range(1, count) if counts[i] < largest] or [i for i in range(1, count) if counts[i] < most]
        pool, budget = sum([portions[i] for i in candidates]), rest
        for i in candidates:
            extra = min(most - counts[i], max(1, budget * portions[i] // pool), rest)
            counts[i] = counts[i] + extra
            rest = rest - extra
    return np.array(counts)


def bell_draw(key, extent, deviation, reach, shards=(), held_as=jnp.bfloat16):
    factor_of = block_scale(key, extent, shards, -0.22, 0.18) if shards else 1.0
    values = jax.random.normal(key, extent, jnp.float32) * deviation * factor_of
    return jnp.minimum(jnp.maximum(values, -reach), reach).astype(held_as)


def setup_inputs(seed: int = 0, part: int = 0) -> dict:
    arg_keys = jax.random.split(jax.random.key(seed), 10)
    part_keys = jax.random.split(jax.random.fold_in(arg_keys[9], part), 10)
    x_tokens = bell_draw(part_keys[0], (TOKENS, D), 1.0, 6.0, ((0, 16),))
    grad_values = bell_draw(part_keys[1], (TOKENS, D), 1.0, 6.0, ((0, 16),))
    grad_scale = jnp.clip(jnp.exp(math.log(1.0) - 2.9957323 * jax.random.uniform(part_keys[2], (TOKENS,), jnp.float32) ** block_scale(part_keys[2], (TOKENS,), ((0, 16),), -0.2, 0.2)), 0.05, 1.0)
    combine = jnp.clip(0.1 + 0.79999997 * jax.random.uniform(part_keys[3], (TOKENS, 2), jnp.float32) ** block_scale(part_keys[3], (TOKENS, 2), ((0, 16),), -0.2, 0.2), 0.1, 0.9)
    routes_keys = jax.random.split(jax.random.fold_in(part_keys[4], 1), TOKENS // TOK_DEV)
    routes_turns = jax.random.permutation(jax.random.fold_in(part_keys[4], 3), TOKENS // TOK_DEV)
    routes = jax.vmap(lambda own, number: routed_block(jax.random.fold_in(part_keys[4], 2), own, number, TOK_DEV, EXPERTS, 2, MOST, 2))(routes_keys, routes_turns).reshape((TOKENS, 2))
    pattern = plant(jax.random.randint(arg_keys[5], (EXPERTS, GROUPS), 0, 6), jax.random.fold_in(arg_keys[5], 1), 0, 5).astype(jnp.int32)
    w_gate = bell_draw(arg_keys[6], (KEPT, EXPERTS * FF), KEPT ** -0.5, 0.15625, ((1, 16),))
    w_up = bell_draw(arg_keys[7], (KEPT, EXPERTS * FF), KEPT ** -0.5, 0.15625, ((1, 16),))
    w_down = bell_draw(arg_keys[8], (EXPERTS * FF, KEPT), FF ** -0.5, 0.0625, ((0, 16),))
    return {"x_tokens": x_tokens, "grad_values": grad_values, "grad_scale": grad_scale, "combine": combine, "routes": routes, "pattern": pattern, "w_gate": w_gate, "w_up": w_up, "w_down": w_down}


def kept_columns(pattern):
    pattern_codes = jnp.arange(6, dtype=jnp.int32)
    onehot = (pattern[..., None] == pattern_codes).astype(jnp.int32)
    first_pos = jnp.sum(onehot * jnp.array([0, 0, 0, 1, 1, 2], dtype=jnp.int32), axis=-1, dtype=jnp.int32)
    second_pos = jnp.sum(onehot * jnp.array([1, 2, 3, 2, 3, 3], dtype=jnp.int32), axis=-1, dtype=jnp.int32)
    group_base = 4 * jnp.arange(pattern.shape[-1], dtype=jnp.int32)
    kept_pairs = jnp.stack([group_base + first_pos, group_base + second_pos], axis=-1)
    return kept_pairs.reshape(pattern.shape[0], -1)


def matmul(left, right):
    return jnp.dot(left.astype(jnp.float32), right.astype(jnp.float32), preferred_element_type=jnp.float32)


def reference(x_tokens, grad_values, grad_scale, combine, routes, pattern, w_gate, w_up, w_down):
    kept = kept_columns(pattern)
    grad_sum = jnp.zeros((TOKENS, D), jnp.float32)
    gate_parts = []
    up_parts = []
    down_parts = []
    for expert in range(EXPERTS):
        chosen = (routes == expert).astype(jnp.float32)
        weight = jnp.sum(chosen * combine, axis=1) * grad_scale
        columns = kept[expert]
        rows_in = jnp.take(x_tokens, columns, axis=1)
        rows_grad = (weight[:, None] * jnp.take(grad_values, columns, axis=1).astype(jnp.float32)).astype(jnp.bfloat16)
        gate_block = w_gate[:, expert * FF:(expert + 1) * FF]
        up_block = w_up[:, expert * FF:(expert + 1) * FF]
        down_block = w_down[expert * FF:(expert + 1) * FF, :]
        gate_pre = matmul(rows_in, gate_block)
        up_pre = matmul(rows_in, up_block)
        sigmoid_gate = jax.nn.sigmoid(gate_pre)
        silu_gate = gate_pre * sigmoid_gate
        hidden = (silu_gate * up_pre).astype(jnp.bfloat16)
        grad_hidden = matmul(rows_grad, down_block.T)
        grad_gate_pre = (grad_hidden * up_pre * sigmoid_gate * (1.0 + gate_pre * (1.0 - sigmoid_gate))).astype(jnp.bfloat16)
        grad_up_pre = (grad_hidden * silu_gate).astype(jnp.bfloat16)
        down_parts.append(matmul(hidden.T, rows_grad).astype(jnp.bfloat16))
        gate_parts.append(matmul(rows_in.T, grad_gate_pre).astype(jnp.bfloat16))
        up_parts.append(matmul(rows_in.T, grad_up_pre).astype(jnp.bfloat16))
        back_rows = matmul(grad_gate_pre, gate_block.T)
        back_rows = back_rows + matmul(grad_up_pre, up_block.T)
        grad_sum = grad_sum.at[:, columns].add(back_rows)
    grad_tokens = grad_sum.astype(jnp.bfloat16)
    grad_gate = jnp.concatenate(gate_parts, axis=1)
    grad_up = jnp.concatenate(up_parts, axis=1)
    grad_down = jnp.concatenate(down_parts, axis=0)
    return (grad_tokens, grad_gate, grad_up, grad_down)
```

```python
import functools

import jax
import jax.numpy as jnp
from jax import lax
from jax.experimental import pallas as pl
from jax.experimental.pallas import tpu as pltpu
from jax.sharding import PartitionSpec as P

MOST = 5
LANES = 128
SUB = 8
F32 = jnp.float32
BF16 = jnp.bfloat16
VMEM = pl.BlockSpec(memory_space=pltpu.VMEM)
SMEM = pl.BlockSpec(memory_space=pltpu.SMEM)
ANY = pl.BlockSpec(memory_space=pl.ANY)


def vmem(shape, dtype):
    return pltpu.VMEM(shape, dtype)


def params(mib=48):
    return pltpu.CompilerParams(vmem_limit_bytes=mib << 20)


def cost(flops, bytes_accessed):
    return pl.CostEstimate(flops=int(flops), bytes_accessed=int(bytes_accessed), transcendentals=0)


def block_rows(chunks):
    return -(-((chunks - 1) * MOST + SUB) // 16) * 16


def iotas():
    lane = lax.broadcasted_iota(jnp.int32, (SUB, LANES), 1)
    sub = lax.broadcasted_iota(jnp.int32, (SUB, LANES), 0)
    return lane, sub


def lanes_of(values, index):
    return jnp.take_along_axis(values, index, axis=1, mode="promise_in_bounds")


def rows_of(values, index):
    return jnp.take_along_axis(values, index, axis=0, mode="promise_in_bounds")


def positions(code):
    first = (code >= 3).astype(jnp.int32) + (code >= 5).astype(jnp.int32)
    second = jnp.where(code < 3, code + 1, jnp.where(code < 5, code - 1, 3))
    return first, second


def expert_pattern(pattern_ref, expert, chunks):
    parts = []
    for part in range(-(-chunks // 2)):
        at = slice(part * LANES, (part + 1) * LANES)
        row = pattern_ref[0:1, at]
        for other in range(1, pattern_ref.shape[0]):
            row = jnp.where(expert == other, pattern_ref[other : other + 1, at], row)
        parts.append(jnp.broadcast_to(row, (SUB, LANES)))
    return parts


def hits(routes_ref, token, expert):
    first = routes_ref[token, 0] == expert
    second = routes_ref[token, 1] == expert
    return first, jnp.logical_or(first, second)


def dispatch_kernel(
    routes_ref, combine_ref, scale_ref, pattern_ref, x_ref, g_ref, *rest, n_e, holders, chunks
):
    outs, (slot_token, slot_weight, stage) = rest[:n_e], rest[n_e:]
    toks = x_ref.shape[0]
    block = block_rows(chunks)
    me = lax.axis_index("expert")
    lane, sub = iotas()
    stage[block - SUB : block, :] = jnp.zeros((SUB, LANES), F32)
    stage[2 * block - SUB : 2 * block, :] = jnp.zeros((SUB, LANES), F32)
    for k in range(n_e):
        expert = jnp.bitwise_xor(me, k) // holders
        count = jnp.int32(0)
        for token in range(toks):
            first, hit = hits(routes_ref, token, expert)
            weight = jnp.where(first, combine_ref[token, 0], combine_ref[token, 1])
            slot_token[count] = jnp.int32(token)
            slot_weight[count] = weight * scale_ref[token]
            count = count + hit.astype(jnp.int32)
        index = jnp.zeros((SUB, LANES), jnp.int32)
        weight = jnp.zeros((SUB, LANES), F32)
        for slot in range(MOST):
            filled = slot < count
            token = jnp.where(filled, slot_token[slot], 0)
            coef = jnp.where(filled, slot_weight[slot], 0.0)
            index = jnp.where(sub == slot, token, index)
            weight = jnp.where(sub == slot, coef, weight)
        valid = sub < count
        codes = expert_pattern(pattern_ref, expert, chunks)
        for c in range(chunks):
            code = lanes_of(
                codes[c // 2], lane // 2 + (c % 2) * (LANES // 2)
            )
            first, second = positions(code)
            source = 4 * (lane // 2) + jnp.where(lane % 2 == 0, first, second)
            local = jnp.bitwise_and(source, LANES - 1)
            low = lane < LANES // 2
            for ref, base in ((x_ref, 0), (g_ref, block)):
                left = ref[:, 2 * c * LANES : (2 * c + 1) * LANES].astype(F32)
                right = ref[:, (2 * c + 1) * LANES : (2 * c + 2) * LANES].astype(F32)
                picked = jnp.where(low, lanes_of(left, local), lanes_of(right, local))
                picked = rows_of(picked, index)
                if base:
                    picked = picked * weight
                picked = jnp.where(valid, picked, 0.0)
                stage[base + c * MOST : base + c * MOST + SUB, :] = picked
        outs[k][...] = stage[...].astype(BF16)


def dispatch(routes, combine, scale, pattern, x, g, n_e, holders, chunks):
    block = block_rows(chunks)
    toks = x.shape[0]
    return pl.pallas_call(
        functools.partial(dispatch_kernel, n_e=n_e, holders=holders, chunks=chunks),
        out_shape=[vmem((2 * block, LANES), BF16)] * n_e,
        in_specs=[SMEM, SMEM, SMEM, VMEM, VMEM, VMEM],
        out_specs=[VMEM] * n_e,
        scratch_shapes=[
            pltpu.SMEM((toks + 1,), jnp.int32),
            pltpu.SMEM((toks + 1,), F32),
            pltpu.VMEM((2 * block, LANES), F32),
        ],
        compiler_params=params(8),
        name="dispatch",
    )(routes, combine, scale, pattern, x, g)


def join_kernel(*refs, n_e, block):
    ins, (zx, zg) = refs[:n_e], refs[n_e:]
    for k in range(n_e):
        zx[k * block : (k + 1) * block, :] = ins[k][:block, :]
        zg[k * block : (k + 1) * block, :] = ins[k][block:, :]


def join(parts, block):
    n_e = len(parts)
    return pl.pallas_call(
        functools.partial(join_kernel, n_e=n_e, block=block),
        out_shape=[vmem((n_e * block, LANES), BF16)] * 2,
        in_specs=[VMEM] * n_e,
        out_specs=[VMEM] * 2,
        compiler_params=params(8),
        name="join",
    )(*parts)


def load_kernel(wg, wu, wd, after, og, ou, od, sems):
    pieces = 4
    copies = []
    for a, (source, target) in enumerate(((wg, og), (wu, ou), (wd, od))):
        rows = source.shape[0] // pieces
        for i in range(pieces):
            at = pl.ds(i * rows, rows)
            copies.append(pltpu.make_async_copy(source.at[at], target.at[at], sems.at[a, i]))
    for copy in copies:
        copy.start()
    for copy in copies:
        copy.wait()


def load_weights(wg, wu, wd, after):
    size = sum(w.size * 2 for w in (wg, wu, wd))
    return pl.pallas_call(
        load_kernel,
        out_shape=[vmem(w.shape, w.dtype) for w in (wg, wu, wd)],
        in_specs=[ANY] * 4,
        out_specs=[VMEM] * 3,
        scratch_shapes=[pltpu.SemaphoreType.DMA((3, 4))],
        compiler_params=params(32),
        cost_estimate=cost(0, size),
        name="load_weights",
    )(wg, wu, wd, after)


def unpack_rows(arrays, stage, rows_ref, n_e, block, chunks):
    sources = n_e * len(arrays)
    for i, ref in enumerate(arrays):
        stage[i * n_e * block : (i + 1) * n_e * block, :] = ref[...].astype(F32)
    for c in range(chunks):
        for slot in range(MOST):
            picked = stage[pl.ds(c * MOST + slot, sources, stride=block), :]
            rows_ref[slot * sources : (slot + 1) * sources, c * LANES : (c + 1) * LANES] = (
                picked.astype(BF16)
            )


def tile_of(size, most):
    return min(size, most)


def forward_kernel(*refs, n_t, n_e, block, chunks):
    arrays, (wg, wu, rows, hidden, slope, silu_out, stage) = refs[:n_t], refs[n_t:]
    unpack_rows(arrays, stage, rows, n_e, block, chunks)
    x = rows[...]
    hid = wg.shape[1]
    tile = tile_of(hid, 256)
    for i in range(hid // tile):
        at = slice(i * tile, (i + 1) * tile)
        gate = jnp.dot(x, wg[:, at], preferred_element_type=F32)
        up = jnp.dot(x, wu[:, at], preferred_element_type=F32)
        sig = jax.nn.sigmoid(gate)
        silu = gate * sig
        hidden[:, at] = (silu * up).astype(BF16)
        slope[:, at] = up * sig * (1.0 + gate * (1.0 - sig))
        silu_out[:, at] = silu


def forward(arrays, wg, wu, n_e, block, chunks):
    n_t = len(arrays)
    count = MOST * n_e * n_t
    kept, hid = wg.shape
    return pl.pallas_call(
        functools.partial(forward_kernel, n_t=n_t, n_e=n_e, block=block, chunks=chunks),
        out_shape=[
            vmem((count, kept), BF16),
            vmem((count, hid), BF16),
            vmem((count, hid), F32),
            vmem((count, hid), F32),
        ],
        in_specs=[VMEM] * (n_t + 2),
        out_specs=[VMEM] * 4,
        scratch_shapes=[pltpu.VMEM((n_t * n_e * block, LANES), F32)],
        compiler_params=params(),
        cost_estimate=cost(4 * 4 * count * kept * hid, 4 * kept * hid),
        name="forward",
    )(*arrays, wg, wu)


def backward_kernel(*refs, n_t, n_e, block, chunks):
    arrays, (slope, silu, wg, wu, wd), rest = refs[:n_t], refs[n_t : n_t + 5], refs[n_t + 5 :]
    (rows, d_gate, d_up), outs, (stage, total) = rest[:3], rest[3 : 3 + n_t], rest[3 + n_t :]
    unpack_rows(arrays, stage, rows, n_e, block, chunks)
    last = (((1,), (1,)), ((), ()))
    hid, kept = wd.shape
    tile = tile_of(hid, 256)
    g = rows[...]
    for i in range(hid // tile):
        at = slice(i * tile, (i + 1) * tile)
        grad = lax.dot_general(g, wd[at, :], last, preferred_element_type=F32)
        d_gate[:, at] = (grad * slope[:, at]).astype(BF16)
        d_up[:, at] = (grad * silu[:, at]).astype(BF16)
    sources = n_e * n_t
    for row in range(chunks * MOST, block):
        stage[pl.ds(row, sources, stride=block), :] = jnp.zeros((sources, LANES), F32)
    dg, du = d_gate[...], d_up[...]
    width = 2 * LANES if kept % (2 * LANES) == 0 else LANES
    for i in range(kept // width):
        at = slice(i * width, (i + 1) * width)
        back = lax.dot_general(dg, wg[at, :], last, preferred_element_type=F32)
        back = back + lax.dot_general(du, wu[at, :], last, preferred_element_type=F32)
        for half in range(width // LANES):
            c = i * (width // LANES) + half
            for slot in range(MOST):
                stage[pl.ds(c * MOST + slot, sources, stride=block), :] = back[
                    slot * sources : (slot + 1) * sources, half * LANES : (half + 1) * LANES
                ]
    for i in range(n_t):
        outs[i][...] = stage[i * n_e * block : (i + 1) * n_e * block, :].astype(BF16)


def backward(arrays, slope, silu, wg, wu, wd, n_e, block, chunks):
    n_t = len(arrays)
    count = MOST * n_e * n_t
    kept, hid = wg.shape
    return pl.pallas_call(
        functools.partial(backward_kernel, n_t=n_t, n_e=n_e, block=block, chunks=chunks),
        out_shape=[
            vmem((count, kept), BF16),
            vmem((count, hid), BF16),
            vmem((count, hid), BF16),
        ]
        + [vmem((n_e * block, LANES), BF16)] * n_t,
        in_specs=[VMEM] * (n_t + 5),
        out_specs=[VMEM] * (3 + n_t),
        scratch_shapes=[
            pltpu.VMEM((n_t * n_e * block, LANES), F32),
            pltpu.VMEM((SUB, LANES), F32),
        ],
        compiler_params=params(),
        cost_estimate=cost(6 * 4 * count * kept * hid, 6 * kept * hid),
        name="backward",
    )(*arrays, slope, silu, wg, wu, wd)


def outer_kernel(left, *refs):
    rights, outs = refs[: len(refs) // 2], refs[len(refs) // 2 :]
    first = (((0,), (0,)), ((), ()))
    for right, out in zip(rights, outs):
        out[...] = lax.dot_general(left[...], right[...], first, preferred_element_type=F32).astype(
            BF16
        )


def outer(left, rights, name):
    count, m = left.shape
    n = rights[0].shape[1]
    tile = tile_of(m, 256)
    return pl.pallas_call(
        outer_kernel,
        grid=(m // tile,),
        out_shape=[jax.ShapeDtypeStruct((m, n), BF16)] * len(rights),
        in_specs=[pl.BlockSpec((count, tile), lambda i: (0, i))]
        + [pl.BlockSpec((count, n), lambda i: (0, 0))] * len(rights),
        out_specs=[pl.BlockSpec((tile, n), lambda i: (i, 0))] * len(rights),
        compiler_params=params(24),
        cost_estimate=cost(2 * 256 * m * n * len(rights), 2 * m * n * len(rights)),
        name=name,
    )(left, *rights)


def sum_kernel(*refs, n_t, n_e, block):
    ins, outs = refs[:n_t], refs[n_t:]
    for k in range(n_e):
        at = slice(k * block, (k + 1) * block)
        total = ins[0][at, :].astype(F32)
        for ref in ins[1:]:
            total = total + ref[at, :].astype(F32)
        outs[k][...] = total.astype(BF16)


def sum_parts(arrays, n_e, block):
    n_t = len(arrays)
    return pl.pallas_call(
        functools.partial(sum_kernel, n_t=n_t, n_e=n_e, block=block),
        out_shape=[vmem((block, LANES), BF16)] * n_e,
        in_specs=[VMEM] * n_t,
        out_specs=[VMEM] * n_e,
        compiler_params=params(8),
        name="sum_parts",
    )(*arrays)


def combine_kernel(routes_ref, pattern_ref, *rest, n_e, holders, chunks):
    ins, (out, stage, total) = rest[:n_e], rest[n_e:]
    toks = out.shape[0]
    me = lax.axis_index("expert")
    lane, sub = iotas()
    for k in range(n_e):
        expert = jnp.bitwise_xor(me, k) // holders
        stage[...] = ins[k][...].astype(F32)
        count = jnp.int32(0)
        slot = jnp.full((SUB, LANES), MOST, jnp.int32)
        for token in range(toks):
            _, hit = hits(routes_ref, token, expert)
            slot = jnp.where(sub == token, jnp.where(hit, count, MOST), slot)
            count = count + hit.astype(jnp.int32)
        valid = slot < MOST
        index = jnp.where(valid, slot, 0)
        codes = expert_pattern(pattern_ref, expert, chunks)
        for c in range(chunks):
            rows = stage[c * MOST : c * MOST + SUB, :]
            rows = jnp.where(valid, rows_of(rows, index), 0.0)
            for half in range(2):
                m = 2 * c + half
                code = lanes_of(
                    codes[m // 4], lane // 4 + (m % 4) * (LANES // 4)
                )
                first, second = positions(code)
                place = lane % 4
                later = place == second
                keep = jnp.logical_or(place == first, later)
                local = half * (LANES // 2) + 2 * (lane // 4) + later.astype(jnp.int32)
                spread = jnp.where(keep, lanes_of(rows, local), 0.0)
                at = slice(m * LANES, (m + 1) * LANES)
                if k == 0:
                    total[:, at] = spread
                elif k < n_e - 1:
                    total[:, at] += spread
                else:
                    out[:, at] = (total[:, at] + spread).astype(BF16)


def combine_rows(routes, pattern, arrays, toks, width, holders, chunks):
    n_e = len(arrays)
    block = arrays[0].shape[0]
    return pl.pallas_call(
        functools.partial(combine_kernel, n_e=n_e, holders=holders, chunks=chunks),
        out_shape=jax.ShapeDtypeStruct((toks, width), BF16),
        in_specs=[SMEM, VMEM] + [VMEM] * n_e,
        out_specs=VMEM,
        scratch_shapes=[pltpu.VMEM((block, LANES), F32), pltpu.VMEM((toks, width), F32)],
        compiler_params=params(8),
        name="combine_rows",
    )(routes, pattern, *arrays)


def swap(value, axis, k):
    size = lax.axis_size(axis)
    return lax.ppermute(value, axis, [(i, i ^ k) for i in range(size)])


def body(x_tokens, grad_values, grad_scale, combine, routes, pattern, w_gate, w_up, w_down):
    n_e = lax.axis_size("expert")
    n_t = lax.axis_size("tensor")
    experts = pattern.shape[0]
    holders = n_e // experts
    toks, width = x_tokens.shape
    chunks = w_gate.shape[0] // LANES
    block = block_rows(chunks)

    sent = dispatch(
        routes, combine, grad_scale, pattern, x_tokens, grad_values, n_e, holders, chunks
    )
    parts = [sent[0]] + [swap(sent[k], "expert", k) for k in range(1, n_e)]
    zx, zg = join(parts, block)
    all_x = [zx] + [swap(zx, "tensor", k) for k in range(1, n_t)]
    all_g = [zg] + [swap(zg, "tensor", k) for k in range(1, n_t)]
    wg, wu, wd = load_weights(w_gate, w_up, w_down, zx)
    rows_in, hidden, slope, silu = forward(all_x, wg, wu, n_e, block, chunks)
    rows_grad, d_gate, d_up, *back = backward(all_g, slope, silu, wg, wu, wd, n_e, block, chunks)
    back = [back[0]] + [swap(back[k], "tensor", k) for k in range(1, n_t)]
    part_gate, part_up = outer(rows_in, [d_gate, d_up], "grads_in")
    summed = sum_parts(back, n_e, block)
    summed = [summed[0]] + [swap(summed[k], "expert", k) for k in range(1, n_e)]
    (part_down,) = outer(hidden, [rows_grad], "grads_out")
    grad_tokens = combine_rows(routes, pattern, summed, toks, width, holders, chunks)
    return grad_tokens, part_gate, part_up, part_down


def solution(mesh):
    in_specs = (
        P(("group", "expert", "tensor"), None),
        P(("group", "expert", "tensor"), None),
        P(("group", "expert", "tensor")),
        P(("group", "expert", "tensor"), None),
        P(("group", "expert", "tensor"), None),
        P(),
        P(None, ("expert", "tensor")),
        P(None, ("expert", "tensor")),
        P(("expert", "tensor"), None),
    )
    out_specs = (
        P(("group", "expert", "tensor"), None),
        P("group", ("expert", "tensor")),
        P("group", ("expert", "tensor")),
        P(("expert", "tensor"), "group"),
    )
    return jax.shard_map(body, mesh=mesh, in_specs=in_specs, out_specs=out_specs, check_vma=False)
```

```python
import functools

import jax
import jax.numpy as jnp
from jax import lax
from jax.experimental import pallas as pl
from jax.experimental.pallas import tpu as pltpu
from jax.sharding import PartitionSpec as P

MOST = 5
LANES = 128
SUB = 8
PIECES = 4
DISPATCH_MIB = 56
F32 = jnp.float32
BF16 = jnp.bfloat16
VMEM = pl.BlockSpec(memory_space=pltpu.VMEM)
SMEM = pl.BlockSpec(memory_space=pltpu.SMEM)
ANY = pl.BlockSpec(memory_space=pl.ANY)


def vmem(shape, dtype):
    return pltpu.VMEM(shape, dtype)


def params(mib=48):
    return pltpu.CompilerParams(vmem_limit_bytes=mib << 20)


def cost(flops, bytes_accessed):
    return pl.CostEstimate(flops=int(flops), bytes_accessed=int(bytes_accessed), transcendentals=0)


def block_rows(chunks):
    return -(-((chunks - 1) * MOST + SUB) // 16) * 16


def iotas():
    lane = lax.broadcasted_iota(jnp.int32, (SUB, LANES), 1)
    sub = lax.broadcasted_iota(jnp.int32, (SUB, LANES), 0)
    return lane, sub


def lanes_of(values, index):
    return jnp.take_along_axis(values, index, axis=1, mode="promise_in_bounds")


def positions(code):
    first = (code >= 3).astype(jnp.int32) + (code >= 5).astype(jnp.int32)
    second = jnp.where(code < 3, code + 1, jnp.where(code < 5, code - 1, 3))
    return first, second


def pattern_rows(pattern_ref, table, parts):
    experts = pattern_ref.shape[0]
    table[...] = jnp.zeros(table.shape, table.dtype)
    for part in range(parts):
        table[part * SUB : part * SUB + experts, :] = pattern_ref[
            :, part * LANES : (part + 1) * LANES
        ]


def row_copies(source, target, sems):
    rows = source.shape[0] // PIECES
    return [
        pltpu.make_async_copy(
            source.at[pl.ds(i * rows, rows)], target.at[pl.ds(i * rows, rows)], sems.at[i]
        )
        for i in range(PIECES)
    ]


def load_kernel(w_ref, after, w_out, sems):
    loads = row_copies(w_ref, w_out, sems)
    for load in loads:
        load.start()
    for load in loads:
        load.wait()


def load_weights(weights, after):
    return pl.pallas_call(
        load_kernel,
        out_shape=vmem(weights.shape, weights.dtype),
        in_specs=[ANY] * 2,
        out_specs=VMEM,
        scratch_shapes=[pltpu.SemaphoreType.DMA((PIECES,))],
        compiler_params=params(4),
        cost_estimate=cost(0, 2 * weights.size),
        name="load_weights",
    )(weights, after)


def dispatch_kernel(
    routes_any, combine_any, scale_any, pattern_any, x_any, g_any, w_any, *rest, n_e, holders, chunks
):
    outs, rest = rest[:n_e], rest[n_e:]
    w_out, routes, weights, scale, count, pattern, x_in, g_in, codes = rest[:9]
    x_rows, g_rows, index, stage, in_sems, sems = rest[9:]
    moves = [
        pltpu.make_async_copy(source, target, in_sems.at[i])
        for i, (source, target) in enumerate(
            (
                (pattern_any, pattern),
                (routes_any, routes),
                (combine_any, weights),
                (scale_any, scale),
                (x_any, x_in),
                (g_any, g_in),
            )
        )
    ]
    for move in moves:
        move.start()
    loads = row_copies(w_any, w_out, sems)
    for load in loads:
        load.start()
    experts, toks = pattern.shape[0], x_in.shape[0]
    parts = chunks // 2
    block, region = block_rows(chunks), region_rows()
    me = lax.axis_index("expert")
    lane, _ = iotas()
    stage[...] = jnp.zeros(stage.shape, F32)
    moves[0].wait()
    pattern_rows(pattern, codes, parts)
    for expert in range(experts):
        count[expert] = jnp.int32(0)
        own = codes[pl.ds(expert, SUB, stride=SUB), :]
        for odd in range(2):
            first, second = positions(lanes_of(own, lane // 2 + odd * (LANES // 2)))
            source = 4 * (lane // 2) + jnp.where(lane % 2 == 0, first, second)
            index[expert * 2 + odd] = jnp.bitwise_and(source, LANES - 1)
    for move in moves[1:]:
        move.wait()
    for ref, rows in ((x_in, x_rows), (g_in, g_rows)):
        for m in range(2 * chunks):
            rows[m * SUB : (m + 1) * SUB, :] = ref[:, m * LANES : (m + 1) * LANES].astype(F32)
        rows[2 * chunks * SUB :, :] = jnp.zeros((rows.shape[0] - 2 * chunks * SUB, LANES), F32)
    low = lane < LANES // 2
    for token in range(toks):
        for choice in range(2):
            expert = routes[choice, token]
            slot = count[expert]
            count[expert] = slot + 1
            weight = weights[choice, token] * scale[token]
            for odd in range(2):
                local = index[expert * 2 + odd]
                for array, rows in ((0, x_rows), (1, g_rows)):
                    left = rows[pl.ds(2 * odd * SUB + token, SUB, stride=4 * SUB), :]
                    right = rows[pl.ds((2 * odd + 1) * SUB + token, SUB, stride=4 * SUB), :]
                    picked = jnp.where(low, lanes_of(left, local), lanes_of(right, local))
                    if array:
                        picked = picked * weight
                    at = (expert * 2 + array) * region + slot + odd * MOST
                    stage[pl.ds(at, SUB, stride=2 * MOST), :] = picked
    for k in range(n_e):
        expert = jnp.bitwise_xor(me, k) // holders
        for array in range(2):
            at = pl.multiple_of((expert * 2 + array) * region, 16)
            outs[k][array * block : (array + 1) * block, :] = stage[pl.ds(at, block), :].astype(
                BF16
            )
    for load in loads:
        load.wait()


def region_rows():
    return -(-((SUB - 1) * 2 * MOST + 2 * MOST) // 16) * 16


def dispatch(routes, combine, scale, pattern, x, g, weights, n_e, holders, chunks):
    block, region = block_rows(chunks), region_rows()
    experts, toks = pattern.shape[0], x.shape[0]
    return pl.pallas_call(
        functools.partial(dispatch_kernel, n_e=n_e, holders=holders, chunks=chunks),
        out_shape=[vmem((2 * block, LANES), BF16)] * n_e + [vmem(weights.shape, weights.dtype)],
        in_specs=[ANY] * 7,
        out_specs=[VMEM] * (n_e + 1),
        scratch_shapes=[
            pltpu.SMEM(routes.shape, jnp.int32),
            pltpu.SMEM(combine.shape, F32),
            pltpu.SMEM(scale.shape, F32),
            pltpu.SMEM((experts,), jnp.int32),
            pltpu.VMEM(pattern.shape, jnp.int32),
            pltpu.VMEM(x.shape, BF16),
            pltpu.VMEM(g.shape, BF16),
            pltpu.VMEM((SUB * SUB, LANES), jnp.int32),
            pltpu.VMEM((4 * SUB * SUB, LANES), F32),
            pltpu.VMEM((4 * SUB * SUB, LANES), F32),
            pltpu.VMEM((experts * 2, SUB, LANES), jnp.int32),
            pltpu.VMEM((experts * 2 * region, LANES), F32),
            pltpu.SemaphoreType.DMA((6,)),
            pltpu.SemaphoreType.DMA((PIECES,)),
        ],
        compiler_params=params(DISPATCH_MIB),
        name="dispatch",
    )(routes, combine, scale, pattern, x, g, weights)


def join_kernel(*refs, n_e, block):
    ins, (zx, zg) = refs[:n_e], refs[n_e:]
    for k in range(n_e):
        zx[k * block : (k + 1) * block, :] = ins[k][:block, :]
        zg[k * block : (k + 1) * block, :] = ins[k][block:, :]


def join(parts, block):
    n_e = len(parts)
    return pl.pallas_call(
        functools.partial(join_kernel, n_e=n_e, block=block),
        out_shape=[vmem((n_e * block, LANES), BF16)] * 2,
        in_specs=[VMEM] * n_e,
        out_specs=[VMEM] * 2,
        compiler_params=params(8),
        name="join",
    )(*parts)


def unpack_rows(arrays, stage, rows_ref, n_e, block, chunks):
    sources = n_e * len(arrays)
    for i, ref in enumerate(arrays):
        stage[i * n_e * block : (i + 1) * n_e * block, :] = ref[...].astype(F32)
    for c in range(chunks):
        for slot in range(MOST):
            picked = stage[pl.ds(c * MOST + slot, sources, stride=block), :]
            rows_ref[slot * sources : (slot + 1) * sources, c * LANES : (c + 1) * LANES] = (
                picked.astype(BF16)
            )


def tile_of(size, most):
    return min(size, most)


def forward_kernel(*refs, n_t, n_e, block, chunks):
    arrays, (wg, wu, wd, rows, hidden, slope, silu_out, wd_out, stage, sems) = refs[:n_t], refs[n_t:]
    loads = row_copies(wd, wd_out, sems)
    for load in loads:
        load.start()
    unpack_rows(arrays, stage, rows, n_e, block, chunks)
    x = rows[...]
    hid = wg.shape[1]
    tile = tile_of(hid, 256)
    for i in range(hid // tile):
        at = slice(i * tile, (i + 1) * tile)
        gate = jnp.dot(x, wg[:, at], preferred_element_type=F32)
        up = jnp.dot(x, wu[:, at], preferred_element_type=F32)
        sig = jax.nn.sigmoid(gate)
        silu = gate * sig
        hidden[:, at] = (silu * up).astype(BF16)
        slope[:, at] = up * sig * (1.0 + gate * (1.0 - sig))
        silu_out[:, at] = silu
    for load in loads:
        load.wait()


def forward(arrays, wg, wu, wd, n_e, block, chunks):
    n_t = len(arrays)
    count = MOST * n_e * n_t
    kept, hid = wg.shape
    return pl.pallas_call(
        functools.partial(forward_kernel, n_t=n_t, n_e=n_e, block=block, chunks=chunks),
        out_shape=[
            vmem((count, kept), BF16),
            vmem((count, hid), BF16),
            vmem((count, hid), F32),
            vmem((count, hid), F32),
            vmem(wd.shape, wd.dtype),
        ],
        in_specs=[VMEM] * (n_t + 2) + [ANY],
        out_specs=[VMEM] * 5,
        scratch_shapes=[
            pltpu.VMEM((n_t * n_e * block, LANES), F32),
            pltpu.SemaphoreType.DMA((PIECES,)),
        ],
        compiler_params=params(12),
        cost_estimate=cost(4 * 4 * count * kept * hid, 4 * kept * hid),
        name="forward",
    )(*arrays, wg, wu, wd)


def backward_kernel(*refs, n_t, n_e, block, chunks):
    arrays, (slope, silu, wg, wu, wd), rest = refs[:n_t], refs[n_t : n_t + 5], refs[n_t + 5 :]
    (rows, d_gate, d_up), outs, (stage, total) = rest[:3], rest[3 : 3 + n_t], rest[3 + n_t :]
    unpack_rows(arrays, stage, rows, n_e, block, chunks)
    last = (((1,), (1,)), ((), ()))
    hid, kept = wd.shape
    tile = tile_of(hid, 256)
    g = rows[...]
    for i in range(hid // tile):
        at = slice(i * tile, (i + 1) * tile)
        grad = lax.dot_general(g, wd[at, :], last, preferred_element_type=F32)
        d_gate[:, at] = (grad * slope[:, at]).astype(BF16)
        d_up[:, at] = (grad * silu[:, at]).astype(BF16)
    sources = n_e * n_t
    for row in range(chunks * MOST, block):
        stage[pl.ds(row, sources, stride=block), :] = jnp.zeros((sources, LANES), F32)
    dg, du = d_gate[...], d_up[...]
    width = 2 * LANES if kept % (2 * LANES) == 0 else LANES
    for i in range(kept // width):
        at = slice(i * width, (i + 1) * width)
        back = lax.dot_general(dg, wg[at, :], last, preferred_element_type=F32)
        back = back + lax.dot_general(du, wu[at, :], last, preferred_element_type=F32)
        for half in range(width // LANES):
            c = i * (width // LANES) + half
            for slot in range(MOST):
                stage[pl.ds(c * MOST + slot, sources, stride=block), :] = back[
                    slot * sources : (slot + 1) * sources, half * LANES : (half + 1) * LANES
                ]
    for i in range(n_t):
        outs[i][...] = stage[i * n_e * block : (i + 1) * n_e * block, :].astype(BF16)


def backward(arrays, slope, silu, wg, wu, wd, n_e, block, chunks):
    n_t = len(arrays)
    count = MOST * n_e * n_t
    kept, hid = wg.shape
    return pl.pallas_call(
        functools.partial(backward_kernel, n_t=n_t, n_e=n_e, block=block, chunks=chunks),
        out_shape=[
            vmem((count, kept), BF16),
            vmem((count, hid), BF16),
            vmem((count, hid), BF16),
        ]
        + [vmem((n_e * block, LANES), BF16)] * n_t,
        in_specs=[VMEM] * (n_t + 5),
        out_specs=[VMEM] * (3 + n_t),
        scratch_shapes=[
            pltpu.VMEM((n_t * n_e * block, LANES), F32),
            pltpu.VMEM((SUB, LANES), F32),
        ],
        compiler_params=params(12),
        cost_estimate=cost(6 * 4 * count * kept * hid, 6 * kept * hid),
        name="backward",
    )(*arrays, slope, silu, wg, wu, wd)


def outer_kernel(left, *refs):
    rights, outs = refs[: len(refs) // 2], refs[len(refs) // 2 :]
    first = (((0,), (0,)), ((), ()))
    for right, out in zip(rights, outs):
        out[...] = lax.dot_general(left[...], right[...], first, preferred_element_type=F32).astype(
            BF16
        )


def outer(left, rights, tile, name):
    count, m = left.shape
    n = rights[0].shape[1]
    tile = tile_of(m, tile)
    return pl.pallas_call(
        outer_kernel,
        grid=(m // tile,),
        out_shape=[jax.ShapeDtypeStruct((m, n), BF16)] * len(rights),
        in_specs=[pl.BlockSpec((count, tile), lambda i: (0, i))]
        + [pl.BlockSpec((count, n), lambda i: (0, 0))] * len(rights),
        out_specs=[pl.BlockSpec((tile, n), lambda i: (i, 0))] * len(rights),
        compiler_params=params(20),
        cost_estimate=cost(2 * 256 * m * n * len(rights), 2 * m * n * len(rights)),
        name=name,
    )(left, *rights)


def sum_kernel(*refs, n_t, n_e, block):
    ins, outs = refs[:n_t], refs[n_t:]
    for k in range(n_e):
        at = slice(k * block, (k + 1) * block)
        total = ins[0][at, :].astype(F32)
        for ref in ins[1:]:
            total = total + ref[at, :].astype(F32)
        outs[k][...] = total.astype(BF16)


def sum_parts(arrays, n_e, block):
    n_t = len(arrays)
    return pl.pallas_call(
        functools.partial(sum_kernel, n_t=n_t, n_e=n_e, block=block),
        out_shape=[vmem((block, LANES), BF16)] * n_e,
        in_specs=[VMEM] * n_t,
        out_specs=[VMEM] * n_e,
        compiler_params=params(8),
        name="sum_parts",
    )(*arrays)


def combine_kernel(routes, pattern, *rest, n_e, holders, chunks):
    ins, (out, count, codes, index, stage, spread) = rest[:n_e], rest[n_e:]
    experts, toks = pattern.shape[0], out.shape[0]
    block = ins[0].shape[0]
    me = lax.axis_index("expert")
    lane, _ = iotas()
    for k in range(n_e):
        stage[k * block : (k + 1) * block, :] = ins[k][...].astype(F32)
    tail = stage.shape[0] - n_e * block
    stage[n_e * block :, :] = jnp.zeros((tail, LANES), F32)
    pattern_rows(pattern, codes, chunks // 2)
    for expert in range(experts):
        count[expert] = jnp.int32(0)
        own = codes[pl.ds(expert, SUB, stride=SUB), :]
        for quarter in range(4):
            first, second = positions(lanes_of(own, lane // 4 + quarter * (LANES // 4)))
            place = lane % 4
            later = place == second
            local = (quarter % 2) * (LANES // 2) + 2 * (lane // 4) + later.astype(jnp.int32)
            keep = jnp.logical_or(place == first, later)
            index[expert * 4 + quarter] = jnp.where(keep, local, -1)
    for token in range(toks):
        total = [None] * 4
        for choice in range(2):
            expert = routes[choice, token]
            slot = count[expert]
            count[expert] = slot + 1
            for odd in range(2):
                row = None
                for holder in range(holders):
                    k = jnp.bitwise_xor(me, expert * holders + holder)
                    part = stage[pl.ds(k * block + slot + odd * MOST, SUB, stride=2 * MOST), :]
                    row = part if row is None else row + part
                for half in range(2):
                    quarter = 2 * odd + half
                    local = index[expert * 4 + quarter]
                    value = lanes_of(row, jnp.bitwise_and(local, LANES - 1))
                    value = jnp.where(local >= 0, value, 0.0)
                    total[quarter] = value if choice == 0 else total[quarter] + value
        for quarter in range(4):
            spread[pl.ds(quarter * SUB + token, SUB, stride=4 * SUB), :] = total[quarter]
    for m in range(2 * chunks):
        out[:, m * LANES : (m + 1) * LANES] = spread[m * SUB : (m + 1) * SUB, :].astype(BF16)


def combine_rows(routes, pattern, arrays, toks, width, holders, chunks):
    n_e = len(arrays)
    block = arrays[0].shape[0]
    experts = pattern.shape[0]
    return pl.pallas_call(
        functools.partial(combine_kernel, n_e=n_e, holders=holders, chunks=chunks),
        out_shape=jax.ShapeDtypeStruct((toks, width), BF16),
        in_specs=[SMEM, VMEM] + [VMEM] * n_e,
        out_specs=VMEM,
        scratch_shapes=[
            pltpu.SMEM((experts,), jnp.int32),
            pltpu.VMEM((SUB * SUB, LANES), jnp.int32),
            pltpu.VMEM((experts * 4, SUB, LANES), jnp.int32),
            pltpu.VMEM((n_e * block + region_rows() - block, LANES), F32),
            pltpu.VMEM((4 * SUB * SUB, LANES), F32),
        ],
        compiler_params=params(8),
        name="combine_rows",
    )(routes, pattern, *arrays)


def swap(value, axis, k):
    size = lax.axis_size(axis)
    return lax.ppermute(value, axis, [(i, i ^ k) for i in range(size)])


def body(x_tokens, grad_values, grad_scale, combine, routes, pattern, w_gate, w_up, w_down):
    n_e = lax.axis_size("expert")
    n_t = lax.axis_size("tensor")
    experts = pattern.shape[0]
    holders = n_e // experts
    toks, width = x_tokens.shape
    chunks = w_gate.shape[0] // LANES
    block = block_rows(chunks)

    routes, combine = routes.T, combine.T
    *sent, wg = dispatch(
        routes, combine, grad_scale, pattern, x_tokens, grad_values, w_gate, n_e, holders, chunks
    )
    parts = [sent[0]] + [swap(sent[k], "expert", k) for k in range(1, n_e)]
    wu = load_weights(w_up, sent[0])
    zx, zg = join(parts, block)
    all_x = [zx] + [swap(zx, "tensor", k) for k in range(1, n_t)]
    all_g = [zg] + [swap(zg, "tensor", k) for k in range(1, n_t)]
    rows_in, hidden, slope, silu, wd = forward(all_x, wg, wu, w_down, n_e, block, chunks)
    rows_grad, d_gate, d_up, *back = backward(all_g, slope, silu, wg, wu, wd, n_e, block, chunks)
    back = [back[0]] + [swap(back[k], "tensor", k) for k in range(1, n_t)]
    part_gate, part_up = outer(rows_in, [d_gate, d_up], 512, "grads_in")
    summed = sum_parts(back, n_e, block)
    summed = [summed[0]] + [swap(summed[k], "expert", k) for k in range(1, n_e)]
    (part_down,) = outer(hidden, [rows_grad], 1024, "grads_out")
    grad_tokens = combine_rows(routes, pattern, summed, toks, width, holders, chunks)
    return grad_tokens, part_gate, part_up, part_down


def solution(mesh):
    in_specs = (
        P(("group", "expert", "tensor"), None),
        P(("group", "expert", "tensor"), None),
        P(("group", "expert", "tensor")),
        P(("group", "expert", "tensor"), None),
        P(("group", "expert", "tensor"), None),
        P(),
        P(None, ("expert", "tensor")),
        P(None, ("expert", "tensor")),
        P(("expert", "tensor"), None),
    )
    out_specs = (
        P(("group", "expert", "tensor"), None),
        P("group", ("expert", "tensor")),
        P("group", ("expert", "tensor")),
        P(("expert", "tensor"), "group"),
    )
    return jax.shard_map(body, mesh=mesh, in_specs=in_specs, out_specs=out_specs, check_vma=False)
```

```python
import functools

import jax
import jax.numpy as jnp
from jax import lax
from jax.experimental import pallas as pl
from jax.experimental.pallas import tpu as pltpu
from jax.sharding import PartitionSpec as P

MOST = 5
LANES = 128
SUB = 8
PIECES = 4
TOKEN = (SUB, LANES)
F32 = jnp.float32
BF16 = jnp.bfloat16
VMEM = pl.BlockSpec(memory_space=pltpu.VMEM)
SMEM = pl.BlockSpec(memory_space=pltpu.SMEM)
ANY = pl.BlockSpec(memory_space=pl.ANY)


def vmem(shape, dtype):
    return pltpu.VMEM(shape, dtype)


def in_hbm(value):
    return pltpu.with_memory_space_constraint(value, pltpu.HBM)


def params(mib=48):
    return pltpu.CompilerParams(vmem_limit_bytes=mib << 20)


def cost(flops, bytes_accessed):
    return pl.CostEstimate(flops=int(flops), bytes_accessed=int(bytes_accessed), transcendentals=0)


def block_rows(chunks):
    return -(-((chunks - 1) * MOST + SUB) // 16) * 16


def iotas():
    lane = lax.broadcasted_iota(jnp.int32, (SUB, LANES), 1)
    sub = lax.broadcasted_iota(jnp.int32, (SUB, LANES), 0)
    return lane, sub


def lanes_of(values, index):
    return jnp.take_along_axis(values, index, axis=1, mode="promise_in_bounds")


def positions(code):
    first = (code >= 3).astype(jnp.int32) + (code >= 5).astype(jnp.int32)
    second = jnp.where(code < 3, code + 1, jnp.where(code < 5, code - 1, 3))
    return first, second


def pattern_rows(pattern_ref, table, parts):
    experts = pattern_ref.shape[0]
    table[...] = jnp.zeros(table.shape, table.dtype)
    for part in range(parts):
        table[part * SUB : part * SUB + experts, :] = pattern_ref[
            :, part * LANES : (part + 1) * LANES
        ]


def row_copies(source, target, sems):
    rows = source.shape[0] // PIECES
    return [
        pltpu.make_async_copy(
            source.at[pl.ds(i * rows, rows)], target.at[pl.ds(i * rows, rows)], sems.at[i]
        )
        for i in range(PIECES)
    ]


def dispatch_kernel(
    routes_any, combine_any, scale_any, pattern_any, x_any, g_any, _a, _b, _c, *rest, n_e, holders, chunks
):
    outs, rest = rest[:2], rest[2:]
    routes, weights, scale, count, pattern, x_in, g_in, codes = rest[:8]
    x_rows, g_rows, index, stage, in_sems = rest[8:]
    moves = [
        pltpu.make_async_copy(source, target, in_sems.at[i])
        for i, (source, target) in enumerate(
            (
                (pattern_any, pattern),
                (routes_any, routes),
                (combine_any, weights),
                (scale_any, scale),
                (x_any, x_in),
                (g_any, g_in),
            )
        )
    ]
    for move in moves:
        move.start()
    experts, toks = pattern.shape[0], x_in.shape[0]
    parts = chunks // 2
    block, region = block_rows(chunks), region_rows()
    me = lax.axis_index("expert")
    lane, _ = iotas()
    stage[...] = jnp.zeros(stage.shape, F32)
    moves[0].wait()
    pattern_rows(pattern, codes, parts)
    for expert in range(experts):
        count[expert] = jnp.int32(0)
        own = codes[pl.ds(expert, SUB, stride=SUB), :]
        for odd in range(2):
            first, second = positions(lanes_of(own, lane // 2 + odd * (LANES // 2)))
            source = 4 * (lane // 2) + jnp.where(lane % 2 == 0, first, second)
            index[expert * 2 + odd] = jnp.bitwise_and(source, LANES - 1)
    for move in moves[1:]:
        move.wait()
    for ref, rows in ((x_in, x_rows), (g_in, g_rows)):
        for m in range(2 * chunks):
            rows[m * SUB : (m + 1) * SUB, :] = ref[:, m * LANES : (m + 1) * LANES].astype(F32)
        rows[2 * chunks * SUB :, :] = jnp.zeros((rows.shape[0] - 2 * chunks * SUB, LANES), F32)
    low = lane < LANES // 2
    for token in range(toks):
        for choice in range(2):
            expert = routes[choice, token]
            slot = count[expert]
            count[expert] = slot + 1
            weight = weights[choice, token] * scale[token]
            for odd in range(2):
                local = index[expert * 2 + odd]
                for array, rows in ((0, x_rows), (1, g_rows)):
                    left = rows[pl.ds(2 * odd * SUB + token, SUB, stride=4 * SUB), :]
                    right = rows[pl.ds((2 * odd + 1) * SUB + token, SUB, stride=4 * SUB), :]
                    picked = jnp.where(low, lanes_of(left, local), lanes_of(right, local))
                    if array:
                        picked = picked * weight
                    at = (expert * 2 + array) * region + slot + odd * MOST
                    stage[pl.ds(at, SUB, stride=2 * MOST), :] = picked
    for k in range(n_e):
        expert = jnp.bitwise_xor(me, k) // holders
        for array in range(2):
            at = pl.multiple_of((expert * 2 + array) * region, 16)
            to = (k // 2 * 2 + array) * block
            outs[k % 2][to : to + block, :] = stage[pl.ds(at, block), :].astype(BF16)


def region_rows():
    return -(-((SUB - 1) * 2 * MOST + 2 * MOST) // 16) * 16


def dispatch(routes, combine, scale, pattern, x, g, ws, n_e, holders, chunks):
    block, region = block_rows(chunks), region_rows()
    experts, toks = pattern.shape[0], x.shape[0]
    return pl.pallas_call(
        functools.partial(dispatch_kernel, n_e=n_e, holders=holders, chunks=chunks),
        out_shape=[vmem((n_e * block, LANES), BF16)] * 2,
        in_specs=[ANY] * 9,
        out_specs=[VMEM] * 2,
        scratch_shapes=[
            pltpu.SMEM(routes.shape, jnp.int32),
            pltpu.SMEM(combine.shape, F32),
            pltpu.SMEM(scale.shape, F32),
            pltpu.SMEM((experts,), jnp.int32),
            pltpu.VMEM(pattern.shape, jnp.int32),
            pltpu.VMEM(x.shape, BF16),
            pltpu.VMEM(g.shape, BF16),
            pltpu.VMEM((SUB * SUB, LANES), jnp.int32),
            pltpu.VMEM((4 * SUB * SUB, LANES), F32),
            pltpu.VMEM((4 * SUB * SUB, LANES), F32),
            pltpu.VMEM((experts * 2, SUB, LANES), jnp.int32),
            pltpu.VMEM((experts * 2 * region, LANES), F32),
            pltpu.SemaphoreType.DMA((6,)),
        ],
        compiler_params=params(8),
        name="dispatch",
    )(*(in_hbm(v) for v in (routes, combine, scale, pattern, x, g, *ws)))


def merge_kernel(keep, received, keep_out, send_out, *, run):
    for h in range(keep.shape[0] // run):
        at, to = slice(h * run, (h + 1) * run), h // 2 * 2 * run
        out = send_out if h % 2 else keep_out
        out[to : to + run, :] = keep[at, :]
        out[to + run : to + 2 * run, :] = received[at, :]


def merge(keep, received, run):
    return pl.pallas_call(
        functools.partial(merge_kernel, run=run),
        out_shape=[vmem(keep.shape, BF16)] * 2,
        in_specs=[VMEM] * 2,
        out_specs=[VMEM] * 2,
        compiler_params=params(8),
        name="merge",
    )(keep, received)


def exchange(keep, send, rows):
    n_e = lax.axis_size("expert")
    bit = 1
    while True:
        received = swap(send, "expert", bit)
        if 2 * bit >= n_e:
            return keep, received
        keep, send = merge(keep, received, bit * rows)
        bit *= 2


def join_kernel(keep, received, zx, zg, stage, *, n_e, block, dense):
    for array, out in enumerate((zx, zg)):
        for k in range(n_e):
            half, at = divmod(k, n_e // 2)
            at = (2 * at + array) * block
            source = (keep, received)[half]
            stage[k * dense : k * dense + block, :] = source[at : at + block, :].astype(F32)
        out[...] = stage[: n_e * dense, :].astype(BF16)


def join(keep, received, n_e, block, dense):
    return pl.pallas_call(
        functools.partial(join_kernel, n_e=n_e, block=block, dense=dense),
        out_shape=[vmem((n_e * dense, LANES), BF16)] * 2,
        in_specs=[VMEM] * 2,
        out_specs=[VMEM] * 2,
        scratch_shapes=[pltpu.VMEM((n_e * dense + block, LANES), F32)],
        compiler_params=params(8),
        name="join",
    )(keep, received)


def unpack_rows(arrays, stage, rows_ref, n_e, block, chunks):
    sources = n_e * len(arrays)
    for i, ref in enumerate(arrays):
        stage[i * n_e * block : (i + 1) * n_e * block, :] = ref[...].astype(F32)
    for c in range(chunks):
        for slot in range(MOST):
            picked = stage[pl.ds(c * MOST + slot, sources, stride=block), :]
            rows_ref[slot * sources : (slot + 1) * sources, c * LANES : (c + 1) * LANES] = (
                picked.astype(BF16)
            )


def tile_of(size, most):
    return min(size, most)


def forward_kernel(*refs, n_t, n_e, block, chunks):
    arrays, refs = refs[:n_t], refs[n_t:]
    (wg, wu), (rows, hidden, slope, silu_out), held = refs[:2], refs[2:6], refs[6:8]
    stage, sems = refs[8:]
    loads = []
    for i, (source, target) in enumerate(zip((wg, wu), held)):
        loads += row_copies(source, target, sems.at[i])
    for load in loads:
        load.start()
    unpack_rows(arrays, stage, rows, n_e, block, chunks)
    x = rows[...]
    hid = wg.shape[1]
    tile = tile_of(hid, 256)
    for i in range(hid // tile):
        at = slice(i * tile, (i + 1) * tile)
        gate = jnp.dot(x, wg[:, at], preferred_element_type=F32)
        up = jnp.dot(x, wu[:, at], preferred_element_type=F32)
        sig = jax.nn.sigmoid(gate)
        silu = gate * sig
        hidden[:, at] = (silu * up).astype(BF16)
        slope[:, at] = up * sig * (1.0 + gate * (1.0 - sig))
        silu_out[:, at] = silu
    for load in loads:
        load.wait()


def forward(arrays, wg, wu, n_e, block, chunks):
    n_t = len(arrays)
    count = MOST * n_e * n_t
    kept, hid = wg.shape
    return pl.pallas_call(
        functools.partial(forward_kernel, n_t=n_t, n_e=n_e, block=block, chunks=chunks),
        out_shape=[
            vmem((count, kept), BF16),
            vmem((count, hid), BF16),
            vmem((count, hid), F32),
            vmem((count, hid), F32),
            *(vmem(w.shape, w.dtype) for w in (wg, wu)),
        ],
        in_specs=[VMEM] * (n_t + 2),
        out_specs=[VMEM] * 6,
        scratch_shapes=[
            pltpu.VMEM((n_t * n_e * block, LANES), F32),
            pltpu.SemaphoreType.DMA((2, PIECES)),
        ],
        compiler_params=params(12),
        cost_estimate=cost(4 * 4 * count * kept * hid, 4 * kept * hid),
        name="forward",
    )(*arrays, wg, wu)


def backward_kernel(*refs, n_t, n_e, block, chunks):
    arrays, (slope, silu, wg, wu, wd), rest = refs[:n_t], refs[n_t : n_t + 5], refs[n_t + 5 :]
    (rows, d_gate, d_up), outs, stage = rest[:3], rest[3 : 3 + n_t], rest[3 + n_t]
    unpack_rows(arrays, stage, rows, n_e, block, chunks)
    last = (((1,), (1,)), ((), ()))
    hid, kept = wd.shape
    tile = tile_of(hid, 256)
    g = rows[...]
    for i in range(hid // tile):
        at = slice(i * tile, (i + 1) * tile)
        grad = lax.dot_general(g, wd[at, :], last, preferred_element_type=F32)
        d_gate[:, at] = (grad * slope[:, at]).astype(BF16)
        d_up[:, at] = (grad * silu[:, at]).astype(BF16)
    sources = n_e * n_t
    dg, du = d_gate[...], d_up[...]
    width = 2 * LANES if kept % (2 * LANES) == 0 else LANES
    for i in range(kept // width):
        at = slice(i * width, (i + 1) * width)
        back = lax.dot_general(dg, wg[at, :], last, preferred_element_type=F32)
        back = back + lax.dot_general(du, wu[at, :], last, preferred_element_type=F32)
        for half in range(width // LANES):
            c = i * (width // LANES) + half
            for slot in range(MOST):
                stage[pl.ds(c * MOST + slot, sources, stride=block), :] = back[
                    slot * sources : (slot + 1) * sources, half * LANES : (half + 1) * LANES
                ]
    for i in range(n_t):
        outs[i][...] = stage[i * n_e * block : (i + 1) * n_e * block, :].astype(BF16)


def backward(arrays, slope, silu, wg, wu, wd, n_e, block, chunks):
    n_t = len(arrays)
    count = MOST * n_e * n_t
    kept, hid = wg.shape
    return pl.pallas_call(
        functools.partial(backward_kernel, n_t=n_t, n_e=n_e, block=block, chunks=chunks),
        out_shape=[
            vmem((count, kept), BF16),
            vmem((count, hid), BF16),
            vmem((count, hid), BF16),
        ]
        + [vmem((n_e * block, LANES), BF16)] * n_t,
        in_specs=[VMEM] * (n_t + 5),
        out_specs=[VMEM] * (3 + n_t),
        scratch_shapes=[pltpu.VMEM((n_t * n_e * block, LANES), F32)],
        compiler_params=params(12),
        cost_estimate=cost(6 * 4 * count * kept * hid, 6 * kept * hid),
        name="backward",
    )(*arrays, slope, silu, wg, wu, wd)


def outer_kernel(left, *refs, count, tile, width):
    rights, outs, token = refs[:count], refs[count : 2 * count], refs[2 * count]
    held, sems = refs[2 * count + 1 :]
    first = (((0,), (0,)), ((), ()))
    token[...] = jnp.zeros(TOKEN, F32)
    m, n = outs[0].shape
    moves = []
    for i in range(m // tile):
        rows = pl.ds(i * tile, tile)
        for array in range(count):
            for j in range(n // width):
                at = slice(j * width, (j + 1) * width)
                value = lax.dot_general(
                    left[:, i * tile : (i + 1) * tile],
                    rights[array][:, at],
                    first,
                    preferred_element_type=F32,
                )
                held[array, rows, at] = value.astype(BF16)
            move = pltpu.make_async_copy(
                held.at[array, rows], outs[array].at[rows], sems.at[array, i]
            )
            move.start()
            moves.append(move)
    for move in moves:
        move.wait()


def outer(left, rights, name):
    rows, m = left.shape
    n = rights[0].shape[1]
    count = len(rights)
    tile, width = tile_of(m, 256), tile_of(n, 512)
    return pl.pallas_call(
        functools.partial(outer_kernel, count=count, tile=tile, width=width),
        out_shape=[jax.ShapeDtypeStruct((m, n), BF16)] * count + [vmem(TOKEN, F32)],
        in_specs=[VMEM] * (1 + count),
        out_specs=[ANY] * count + [VMEM],
        scratch_shapes=[
            pltpu.VMEM((count, m, n), BF16),
            pltpu.SemaphoreType.DMA((count, m // tile)),
        ],
        compiler_params=params(28),
        cost_estimate=cost(2 * 256 * m * n * count, 2 * m * n * count),
        name=name,
    )(left, *rights)


def sum_kernel(*refs, n_t, n_e, block, dense):
    ins, (token, keep, send, stage) = refs[:n_t], refs[n_t:]
    total = ins[0][...].astype(F32)
    for ref in ins[1:]:
        total = total + ref[...].astype(F32)
    stage[: n_e * dense, :] = total
    stage[n_e * dense :, :] = jnp.zeros((stage.shape[0] - n_e * dense, LANES), F32)
    for k in range(n_e):
        out = send if k % 2 else keep
        value = stage[k * dense : k * dense + block, :].astype(BF16)
        out[k // 2 * block : (k // 2 + 1) * block, :] = value


def sum_parts(arrays, token, n_e, block, dense):
    n_t = len(arrays)
    return pl.pallas_call(
        functools.partial(sum_kernel, n_t=n_t, n_e=n_e, block=block, dense=dense),
        out_shape=[vmem((n_e // 2 * block, LANES), BF16)] * 2,
        in_specs=[VMEM] * (n_t + 1),
        out_specs=[VMEM] * 2,
        scratch_shapes=[pltpu.VMEM((n_e * dense + block, LANES), F32)],
        compiler_params=params(8),
        name="sum_parts",
    )(*arrays, token)


def combine_kernel(routes, pattern, *rest, n_e, holders, chunks):
    ins, (out, count, codes, index, stage, spread) = rest[:2], rest[2:]
    experts, toks = pattern.shape[0], out.shape[0]
    block = 2 * ins[0].shape[0] // n_e
    me = lax.axis_index("expert")
    lane, _ = iotas()
    for half, ref in enumerate(ins):
        rows = ref.shape[0]
        stage[half * rows : (half + 1) * rows, :] = ref[...].astype(F32)
    tail = stage.shape[0] - n_e * block
    stage[n_e * block :, :] = jnp.zeros((tail, LANES), F32)
    pattern_rows(pattern, codes, chunks // 2)
    for expert in range(experts):
        count[expert] = jnp.int32(0)
        own = codes[pl.ds(expert, SUB, stride=SUB), :]
        for quarter in range(4):
            first, second = positions(lanes_of(own, lane // 4 + quarter * (LANES // 4)))
            place = lane % 4
            later = place == second
            local = (quarter % 2) * (LANES // 2) + 2 * (lane // 4) + later.astype(jnp.int32)
            keep = jnp.logical_or(place == first, later)
            index[expert * 4 + quarter] = jnp.where(keep, local, -1)
    for token in range(toks):
        total = [None] * 4
        for choice in range(2):
            expert = routes[choice, token]
            slot = count[expert]
            count[expert] = slot + 1
            for odd in range(2):
                row = None
                for holder in range(holders):
                    k = jnp.bitwise_xor(me, expert * holders + holder)
                    part = stage[pl.ds(k * block + slot + odd * MOST, SUB, stride=2 * MOST), :]
                    row = part if row is None else row + part
                for half in range(2):
                    quarter = 2 * odd + half
                    local = index[expert * 4 + quarter]
                    value = lanes_of(row, jnp.bitwise_and(local, LANES - 1))
                    value = jnp.where(local >= 0, value, 0.0)
                    total[quarter] = value if choice == 0 else total[quarter] + value
        for quarter in range(4):
            spread[pl.ds(quarter * SUB + token, SUB, stride=4 * SUB), :] = total[quarter]
    for m in range(2 * chunks):
        out[:, m * LANES : (m + 1) * LANES] = spread[m * SUB : (m + 1) * SUB, :].astype(BF16)


def combine_rows(routes, pattern, arrays, toks, width, n_e, holders, chunks):
    block = 2 * arrays[0].shape[0] // n_e
    experts = pattern.shape[0]
    return pl.pallas_call(
        functools.partial(combine_kernel, n_e=n_e, holders=holders, chunks=chunks),
        out_shape=jax.ShapeDtypeStruct((toks, width), BF16),
        in_specs=[SMEM, VMEM] + [VMEM] * 2,
        out_specs=VMEM,
        scratch_shapes=[
            pltpu.SMEM((experts,), jnp.int32),
            pltpu.VMEM((SUB * SUB, LANES), jnp.int32),
            pltpu.VMEM((experts * 4, SUB, LANES), jnp.int32),
            pltpu.VMEM((n_e * block + region_rows() - block, LANES), F32),
            pltpu.VMEM((4 * SUB * SUB, LANES), F32),
        ],
        compiler_params=params(8),
        name="combine_rows",
    )(routes, pattern, *arrays)


def swap(value, axis, k):
    size = lax.axis_size(axis)
    return lax.ppermute(value, axis, [(i, i ^ k) for i in range(size)])


def gather_line(value):
    held = {0: value}
    bit = lax.axis_size("tensor") // 2
    while bit:
        for k in list(held):
            held[k ^ bit] = swap(held[k], "tensor", bit)
        bit //= 2
    return [held[k] for k in range(len(held))]


def body(x_tokens, grad_values, grad_scale, combine, routes, pattern, w_gate, w_up, w_down):
    n_e = lax.axis_size("expert")
    n_t = lax.axis_size("tensor")
    experts = pattern.shape[0]
    holders = n_e // experts
    toks, width = x_tokens.shape
    chunks = w_gate.shape[0] // LANES
    block = block_rows(chunks)
    dense = chunks * MOST

    routes, combine = routes.T, combine.T
    keep, send = dispatch(
        routes, combine, grad_scale, pattern, x_tokens, grad_values, (w_gate, w_up, w_down), n_e, holders, chunks
    )
    zx, zg = join(*exchange(keep, send, 2 * block), n_e, block, dense)
    all_x, all_g = gather_line(zx), gather_line(zg)
    rows_in, hidden, slope, silu, wg, wu = forward(all_x, w_gate, w_up, n_e, dense, chunks)
    rows_grad, d_gate, d_up, *back = backward(
        all_g, slope, silu, wg, wu, w_down, n_e, dense, chunks
    )
    back = [back[0]] + [swap(back[k], "tensor", k) for k in range(1, n_t)]
    part_gate, part_up, token = outer(rows_in, [d_gate, d_up], "grads_in")
    keep, send = sum_parts(back, token, n_e, block, dense)
    summed = exchange(keep, send, block)
    part_down, _ = outer(hidden, [rows_grad], "grad_down")
    grad_tokens = combine_rows(routes, pattern, summed, toks, width, n_e, holders, chunks)
    return grad_tokens, part_gate, part_up, part_down


def solution(mesh):
    in_specs = (
        P(("group", "expert", "tensor"), None),
        P(("group", "expert", "tensor"), None),
        P(("group", "expert", "tensor")),
        P(("group", "expert", "tensor"), None),
        P(("group", "expert", "tensor"), None),
        P(),
        P(None, ("expert", "tensor")),
        P(None, ("expert", "tensor")),
        P(("expert", "tensor"), None),
    )
    out_specs = (
        P(("group", "expert", "tensor"), None),
        P("group", ("expert", "tensor")),
        P("group", ("expert", "tensor")),
        P(("expert", "tensor"), "group"),
    )
    return jax.shard_map(body, mesh=mesh, in_specs=in_specs, out_specs=out_specs, check_vma=False)
```

```python
import functools

import jax
import jax.numpy as jnp
from jax import lax
from jax.experimental import pallas as pl
from jax.experimental.pallas import tpu as pltpu
from jax.sharding import PartitionSpec as P

MOST = 5
LANES = 128
SUB = 8
PIECES = 4
TOKEN = (SUB, LANES)
F32 = jnp.float32
BF16 = jnp.bfloat16
VMEM = pl.BlockSpec(memory_space=pltpu.VMEM)
SMEM = pl.BlockSpec(memory_space=pltpu.SMEM)
ANY = pl.BlockSpec(memory_space=pl.ANY)


def vmem(shape, dtype):
    return pltpu.VMEM(shape, dtype)


def in_hbm(value):
    return pltpu.with_memory_space_constraint(value, pltpu.HBM)


def params(mib=48):
    return pltpu.CompilerParams(vmem_limit_bytes=mib << 20)


def cost(flops, bytes_accessed):
    return pl.CostEstimate(flops=int(flops), bytes_accessed=int(bytes_accessed), transcendentals=0)


def block_rows(chunks):
    return -(-((chunks - 1) * MOST + SUB) // 16) * 16


def iotas():
    lane = lax.broadcasted_iota(jnp.int32, (SUB, LANES), 1)
    sub = lax.broadcasted_iota(jnp.int32, (SUB, LANES), 0)
    return lane, sub


def lanes_of(values, index):
    return jnp.take_along_axis(values, index, axis=1, mode="promise_in_bounds")


def positions(code):
    first = (code >= 3).astype(jnp.int32) + (code >= 5).astype(jnp.int32)
    second = jnp.where(code < 3, code + 1, jnp.where(code < 5, code - 1, 3))
    return first, second


def pattern_rows(pattern_ref, table, parts):
    experts = pattern_ref.shape[0]
    table[...] = jnp.zeros(table.shape, table.dtype)
    for part in range(parts):
        table[part * SUB : part * SUB + experts, :] = pattern_ref[
            :, part * LANES : (part + 1) * LANES
        ]


def row_copies(source, target, sems):
    rows = source.shape[0] // PIECES
    return [
        pltpu.make_async_copy(
            source.at[pl.ds(i * rows, rows)], target.at[pl.ds(i * rows, rows)], sems.at[i]
        )
        for i in range(PIECES)
    ]


def dispatch_kernel(
    routes_any, combine_any, scale_any, pattern_any, x_any, g_any, _a, _b, _c, *rest, n_e, holders, chunks
):
    outs, rest = rest[:2], rest[2:]
    routes, weights, scale, count, pattern, x_in, g_in, codes = rest[:8]
    x_rows, g_rows, index, stage, in_sems = rest[8:]
    moves = [
        pltpu.make_async_copy(source, target, in_sems.at[i])
        for i, (source, target) in enumerate(
            (
                (pattern_any, pattern),
                (routes_any, routes),
                (combine_any, weights),
                (scale_any, scale),
                (x_any, x_in),
                (g_any, g_in),
            )
        )
    ]
    for move in moves:
        move.start()
    experts, toks = pattern.shape[0], x_in.shape[0]
    parts = chunks // 2
    block, region = block_rows(chunks), region_rows()
    me = lax.axis_index("expert")
    lane, _ = iotas()
    stage[...] = jnp.zeros(stage.shape, F32)
    moves[0].wait()
    pattern_rows(pattern, codes, parts)
    for expert in range(experts):
        count[expert] = jnp.int32(0)
        own = codes[pl.ds(expert, SUB, stride=SUB), :]
        for odd in range(2):
            first, second = positions(lanes_of(own, lane // 2 + odd * (LANES // 2)))
            source = 4 * (lane // 2) + jnp.where(lane % 2 == 0, first, second)
            index[expert * 2 + odd] = jnp.bitwise_and(source, LANES - 1)
    for move in moves[1:]:
        move.wait()
    for ref, rows in ((x_in, x_rows), (g_in, g_rows)):
        for m in range(2 * chunks):
            rows[m * SUB : (m + 1) * SUB, :] = ref[:, m * LANES : (m + 1) * LANES].astype(F32)
        rows[2 * chunks * SUB :, :] = jnp.zeros((rows.shape[0] - 2 * chunks * SUB, LANES), F32)
    low = lane < LANES // 2
    for token in range(toks):
        for choice in range(2):
            expert = routes[choice, token]
            slot = count[expert]
            count[expert] = slot + 1
            weight = weights[choice, token] * scale[token]
            for odd in range(2):
                local = index[expert * 2 + odd]
                for array, rows in ((0, x_rows), (1, g_rows)):
                    left = rows[pl.ds(2 * odd * SUB + token, SUB, stride=4 * SUB), :]
                    right = rows[pl.ds((2 * odd + 1) * SUB + token, SUB, stride=4 * SUB), :]
                    picked = jnp.where(low, lanes_of(left, local), lanes_of(right, local))
                    if array:
                        picked = picked * weight
                    at = (expert * 2 + array) * region + slot + odd * MOST
                    stage[pl.ds(at, SUB, stride=2 * MOST), :] = picked
    for k in range(n_e):
        expert = jnp.bitwise_xor(me, k) // holders
        for array in range(2):
            at = pl.multiple_of((expert * 2 + array) * region, 16)
            to = (k // 2 * 2 + array) * block
            outs[k % 2][to : to + block, :] = stage[pl.ds(at, block), :].astype(BF16)


def region_rows():
    return -(-((SUB - 1) * 2 * MOST + 2 * MOST) // 16) * 16


def dispatch(routes, combine, scale, pattern, x, g, ws, n_e, holders, chunks):
    block, region = block_rows(chunks), region_rows()
    experts, toks = pattern.shape[0], x.shape[0]
    return pl.pallas_call(
        functools.partial(dispatch_kernel, n_e=n_e, holders=holders, chunks=chunks),
        out_shape=[vmem((n_e * block, LANES), BF16)] * 2,
        in_specs=[ANY] * 9,
        out_specs=[VMEM] * 2,
        scratch_shapes=[
            pltpu.SMEM(routes.shape, jnp.int32),
            pltpu.SMEM(combine.shape, F32),
            pltpu.SMEM(scale.shape, F32),
            pltpu.SMEM((experts,), jnp.int32),
            pltpu.VMEM(pattern.shape, jnp.int32),
            pltpu.VMEM(x.shape, BF16),
            pltpu.VMEM(g.shape, BF16),
            pltpu.VMEM((SUB * SUB, LANES), jnp.int32),
            pltpu.VMEM((4 * SUB * SUB, LANES), F32),
            pltpu.VMEM((4 * SUB * SUB, LANES), F32),
            pltpu.VMEM((experts * 2, SUB, LANES), jnp.int32),
            pltpu.VMEM((experts * 2 * region, LANES), F32),
            pltpu.SemaphoreType.DMA((6,)),
        ],
        compiler_params=params(8),
        name="dispatch",
    )(*(in_hbm(v) for v in (routes, combine, scale, pattern, x, g, *ws)))


def merge_kernel(keep, received, keep_out, send_out, *, run):
    for h in range(keep.shape[0] // run):
        at, to = slice(h * run, (h + 1) * run), h // 2 * 2 * run
        out = send_out if h % 2 else keep_out
        out[to : to + run, :] = keep[at, :]
        out[to + run : to + 2 * run, :] = received[at, :]


def merge(keep, received, run):
    return pl.pallas_call(
        functools.partial(merge_kernel, run=run),
        out_shape=[vmem(keep.shape, BF16)] * 2,
        in_specs=[VMEM] * 2,
        out_specs=[VMEM] * 2,
        compiler_params=params(8),
        name="merge",
    )(keep, received)


def exchange(keep, send, rows):
    n_e = lax.axis_size("expert")
    bit = 1
    while True:
        received = swap(send, "expert", bit)
        if 2 * bit >= n_e:
            return keep, received
        keep, send = merge(keep, received, bit * rows)
        bit *= 2


def join_kernel(blocks, out, stage, *, block, dense):
    count = blocks.shape[0] // (2 * block)
    for array in range(2):
        for k in range(count):
            at, to = (2 * k + array) * block, (array * count + k) * dense
            stage[to : to + block, :] = blocks[at : at + block, :].astype(F32)
    out[...] = stage[: 2 * count * dense, :].astype(BF16)


def join(blocks, block, dense):
    rows = blocks.shape[0] // block * dense
    return pl.pallas_call(
        functools.partial(join_kernel, block=block, dense=dense),
        out_shape=vmem((rows, LANES), BF16),
        in_specs=[VMEM],
        out_specs=VMEM,
        scratch_shapes=[pltpu.VMEM((rows + block, LANES), F32)],
        compiler_params=params(8),
        name="join",
    )(blocks)


def unpack_rows(stage, rows_ref, sources, dense, chunks):
    for c in range(chunks):
        for slot in range(MOST):
            picked = stage[pl.ds(c * MOST + slot, sources, stride=dense), :]
            rows_ref[slot * sources : (slot + 1) * sources, c * LANES : (c + 1) * LANES] = (
                picked.astype(BF16)
            )


def tile_of(size, most):
    return min(size, most)


def expert_kernel(*refs, n_t, n_e, dense, chunks):
    near, far, (wg, wu, wd), refs = refs[:n_t], refs[n_t : 2 * n_t], refs[2 * n_t :][:3], refs[2 * n_t + 3 :]
    (rows_in, rows_grad, hidden, d_gate, d_up), outs, (x_stage, g_stage) = refs[:5], refs[5:-2], refs[-2:]
    sources, size = n_e * n_t, n_e // 2 * dense
    for part, arrays in enumerate((near, far)):
        for k, ref in enumerate(arrays):
            value = ref[...].astype(F32)
            at = (2 * k + part) * size
            x_stage[at : at + size, :] = value[:size]
            g_stage[at : at + size, :] = value[size:]
    unpack_rows(x_stage, rows_in, sources, dense, chunks)
    unpack_rows(g_stage, rows_grad, sources, dense, chunks)
    last = (((1,), (1,)), ((), ()))
    hid, kept = wd.shape
    tile = tile_of(hid, 256)
    x, g = rows_in[...], rows_grad[...]
    for i in range(hid // tile):
        at = slice(i * tile, (i + 1) * tile)
        gate = jnp.dot(x, wg[:, at], preferred_element_type=F32)
        up = jnp.dot(x, wu[:, at], preferred_element_type=F32)
        grad = lax.dot_general(g, wd[at, :], last, preferred_element_type=F32)
        sig = jax.nn.sigmoid(gate)
        silu = gate * sig
        hidden[:, at] = (silu * up).astype(BF16)
        d_gate[:, at] = (grad * up * sig * (1.0 + gate * (1.0 - sig))).astype(BF16)
        d_up[:, at] = (grad * silu).astype(BF16)
    dg, du = d_gate[...], d_up[...]
    width = 2 * LANES if kept % (2 * LANES) == 0 else LANES
    for i in range(kept // width):
        at = slice(i * width, (i + 1) * width)
        back = lax.dot_general(dg, wg[at, :], last, preferred_element_type=F32)
        back = back + lax.dot_general(du, wu[at, :], last, preferred_element_type=F32)
        for half in range(width // LANES):
            c = i * (width // LANES) + half
            for slot in range(MOST):
                x_stage[pl.ds(c * MOST + slot, sources, stride=dense), :] = back[
                    slot * sources : (slot + 1) * sources, half * LANES : (half + 1) * LANES
                ]
    for k in range(n_t):
        outs[k][...] = x_stage[2 * k * size : 2 * (k + 1) * size, :].astype(BF16)


def expert_rows(near, far, wg, wu, wd, n_e, dense, chunks):
    n_t = len(near)
    count = MOST * n_e * n_t
    kept, hid = wg.shape
    return pl.pallas_call(
        functools.partial(expert_kernel, n_t=n_t, n_e=n_e, dense=dense, chunks=chunks),
        out_shape=[vmem((count, kept), BF16)] * 2
        + [vmem((count, hid), BF16)] * 3
        + [vmem((n_e * dense, LANES), BF16)] * n_t,
        in_specs=[VMEM] * (2 * n_t + 3),
        out_specs=[VMEM] * (5 + n_t),
        scratch_shapes=[pltpu.VMEM((n_t * n_e * dense, LANES), F32)] * 2,
        compiler_params=params(20),
        cost_estimate=cost(10 * 4 * count * kept * hid, 6 * kept * hid),
        name="expert_rows",
    )(*near, *far, wg, wu, wd)


def outer_kernel(left, *refs, count, tile, width):
    rights, outs, token = refs[:count], refs[count : 2 * count], refs[2 * count]
    held, sems = refs[2 * count + 1 :]
    first = (((0,), (0,)), ((), ()))
    token[...] = jnp.zeros(TOKEN, F32)
    m, n = outs[0].shape
    moves = []
    for i in range(m // tile):
        rows = pl.ds(i * tile, tile)
        for array in range(count):
            for j in range(n // width):
                at = slice(j * width, (j + 1) * width)
                value = lax.dot_general(
                    left[:, i * tile : (i + 1) * tile],
                    rights[array][:, at],
                    first,
                    preferred_element_type=F32,
                )
                held[array, rows, at] = value.astype(BF16)
            move = pltpu.make_async_copy(
                held.at[array, rows], outs[array].at[rows], sems.at[array, i]
            )
            move.start()
            moves.append(move)
    for move in moves:
        move.wait()


def outer(left, rights, name):
    rows, m = left.shape
    n = rights[0].shape[1]
    count = len(rights)
    tile, width = tile_of(m, 256), tile_of(n, 512)
    return pl.pallas_call(
        functools.partial(outer_kernel, count=count, tile=tile, width=width),
        out_shape=[jax.ShapeDtypeStruct((m, n), BF16)] * count + [vmem(TOKEN, F32)],
        in_specs=[VMEM] * (1 + count),
        out_specs=[ANY] * count + [VMEM],
        scratch_shapes=[
            pltpu.VMEM((count, m, n), BF16),
            pltpu.SemaphoreType.DMA((count, m // tile)),
        ],
        compiler_params=params(28),
        cost_estimate=cost(2 * 256 * m * n * count, 2 * m * n * count),
        name=name,
    )(left, *rights)


def sum_kernel(*refs, n_t, n_e, block, dense):
    ins, (token, keep, send, stage) = refs[:n_t], refs[n_t:]
    total = ins[0][...].astype(F32)
    for ref in ins[1:]:
        total = total + ref[...].astype(F32)
    stage[: n_e * dense, :] = total
    stage[n_e * dense :, :] = jnp.zeros((stage.shape[0] - n_e * dense, LANES), F32)
    for k in range(n_e):
        out = send if k % 2 else keep
        value = stage[k * dense : k * dense + block, :].astype(BF16)
        out[k // 2 * block : (k // 2 + 1) * block, :] = value


def sum_parts(arrays, token, n_e, block, dense):
    n_t = len(arrays)
    return pl.pallas_call(
        functools.partial(sum_kernel, n_t=n_t, n_e=n_e, block=block, dense=dense),
        out_shape=[vmem((n_e // 2 * block, LANES), BF16)] * 2,
        in_specs=[VMEM] * (n_t + 1),
        out_specs=[VMEM] * 2,
        scratch_shapes=[pltpu.VMEM((n_e * dense + block, LANES), F32)],
        compiler_params=params(8),
        name="sum_parts",
    )(*arrays, token)


def combine_kernel(routes, pattern, *rest, n_e, holders, chunks):
    ins, (out, count, codes, index, stage, spread) = rest[:2], rest[2:]
    experts, toks = pattern.shape[0], out.shape[0]
    block = 2 * ins[0].shape[0] // n_e
    me = lax.axis_index("expert")
    lane, _ = iotas()
    for half, ref in enumerate(ins):
        rows = ref.shape[0]
        stage[half * rows : (half + 1) * rows, :] = ref[...].astype(F32)
    tail = stage.shape[0] - n_e * block
    stage[n_e * block :, :] = jnp.zeros((tail, LANES), F32)
    pattern_rows(pattern, codes, chunks // 2)
    for expert in range(experts):
        count[expert] = jnp.int32(0)
        own = codes[pl.ds(expert, SUB, stride=SUB), :]
        for quarter in range(4):
            first, second = positions(lanes_of(own, lane // 4 + quarter * (LANES // 4)))
            place = lane % 4
            later = place == second
            local = (quarter % 2) * (LANES // 2) + 2 * (lane // 4) + later.astype(jnp.int32)
            keep = jnp.logical_or(place == first, later)
            index[expert * 4 + quarter] = jnp.where(keep, local, -1)
    for token in range(toks):
        total = [None] * 4
        for choice in range(2):
            expert = routes[choice, token]
            slot = count[expert]
            count[expert] = slot + 1
            for odd in range(2):
                row = None
                for holder in range(holders):
                    k = jnp.bitwise_xor(me, expert * holders + holder)
                    part = stage[pl.ds(k * block + slot + odd * MOST, SUB, stride=2 * MOST), :]
                    row = part if row is None else row + part
                for half in range(2):
                    quarter = 2 * odd + half
                    local = index[expert * 4 + quarter]
                    value = lanes_of(row, jnp.bitwise_and(local, LANES - 1))
                    value = jnp.where(local >= 0, value, 0.0)
                    total[quarter] = value if choice == 0 else total[quarter] + value
        for quarter in range(4):
            spread[pl.ds(quarter * SUB + token, SUB, stride=4 * SUB), :] = total[quarter]
    for m in range(2 * chunks):
        out[:, m * LANES : (m + 1) * LANES] = spread[m * SUB : (m + 1) * SUB, :].astype(BF16)


def combine_rows(routes, pattern, arrays, toks, width, n_e, holders, chunks):
    block = 2 * arrays[0].shape[0] // n_e
    experts = pattern.shape[0]
    return pl.pallas_call(
        functools.partial(combine_kernel, n_e=n_e, holders=holders, chunks=chunks),
        out_shape=jax.ShapeDtypeStruct((toks, width), BF16),
        in_specs=[SMEM, VMEM] + [VMEM] * 2,
        out_specs=VMEM,
        scratch_shapes=[
            pltpu.SMEM((experts,), jnp.int32),
            pltpu.VMEM((SUB * SUB, LANES), jnp.int32),
            pltpu.VMEM((experts * 4, SUB, LANES), jnp.int32),
            pltpu.VMEM((n_e * block + region_rows() - block, LANES), F32),
            pltpu.VMEM((4 * SUB * SUB, LANES), F32),
        ],
        compiler_params=params(8),
        name="combine_rows",
    )(routes, pattern, *arrays)


def swap(value, axis, k):
    size = lax.axis_size(axis)
    return lax.ppermute(value, axis, [(i, i ^ k) for i in range(size)])


def gather_line(value):
    held = {0: value}
    bit = lax.axis_size("tensor") // 2
    while bit:
        for k in list(held):
            held[k ^ bit] = swap(held[k], "tensor", bit)
        bit //= 2
    return [held[k] for k in range(len(held))]


def body(x_tokens, grad_values, grad_scale, combine, routes, pattern, w_gate, w_up, w_down):
    n_e = lax.axis_size("expert")
    n_t = lax.axis_size("tensor")
    experts = pattern.shape[0]
    holders = n_e // experts
    toks, width = x_tokens.shape
    chunks = w_gate.shape[0] // LANES
    block = block_rows(chunks)
    dense = chunks * MOST

    routes, combine = routes.T, combine.T
    keep, send = dispatch(
        routes, combine, grad_scale, pattern, x_tokens, grad_values, (w_gate, w_up, w_down), n_e, holders, chunks
    )
    near, far = (gather_line(join(b, block, dense)) for b in exchange(keep, send, 2 * block))
    rows_in, rows_grad, hidden, d_gate, d_up, *back = expert_rows(
        near, far, w_gate, w_up, w_down, n_e, dense, chunks
    )
    back = [back[0]] + [swap(back[k], "tensor", k) for k in range(1, n_t)]
    part_gate, part_up, token = outer(rows_in, [d_gate, d_up], "grads_in")
    keep, send = sum_parts(back, token, n_e, block, dense)
    summed = exchange(keep, send, block)
    part_down, _ = outer(hidden, [rows_grad], "grad_down")
    grad_tokens = combine_rows(routes, pattern, summed, toks, width, n_e, holders, chunks)
    return grad_tokens, part_gate, part_up, part_down


def solution(mesh):
    in_specs = (
        P(("group", "expert", "tensor"), None),
        P(("group", "expert", "tensor"), None),
        P(("group", "expert", "tensor")),
        P(("group", "expert", "tensor"), None),
        P(("group", "expert", "tensor"), None),
        P(),
        P(None, ("expert", "tensor")),
        P(None, ("expert", "tensor")),
        P(("expert", "tensor"), None),
    )
    out_specs = (
        P(("group", "expert", "tensor"), None),
        P("group", ("expert", "tensor")),
        P("group", ("expert", "tensor")),
        P(("expert", "tensor"), "group"),
    )
    return jax.shard_map(body, mesh=mesh, in_specs=in_specs, out_specs=out_specs, check_vma=False)
```

```python
import functools

import jax
import jax.numpy as jnp
from jax import lax
from jax.experimental import pallas as pl
from jax.experimental.pallas import tpu as pltpu
from jax.sharding import PartitionSpec as P

MOST = 5
LANES = 128
SUB = 8
PIECES = 4
TOKEN = (SUB, LANES)
F32 = jnp.float32
BF16 = jnp.bfloat16
VMEM = pl.BlockSpec(memory_space=pltpu.VMEM)
SMEM = pl.BlockSpec(memory_space=pltpu.SMEM)
ANY = pl.BlockSpec(memory_space=pl.ANY)


def vmem(shape, dtype):
    return pltpu.VMEM(shape, dtype)


def in_hbm(value):
    return pltpu.with_memory_space_constraint(value, pltpu.HBM)


def params(mib=48):
    return pltpu.CompilerParams(vmem_limit_bytes=mib << 20)


def cost(flops, bytes_accessed):
    return pl.CostEstimate(flops=int(flops), bytes_accessed=int(bytes_accessed), transcendentals=0)


def block_rows(chunks):
    return -(-((chunks - 1) * MOST + SUB) // 16) * 16


def iotas():
    lane = lax.broadcasted_iota(jnp.int32, (SUB, LANES), 1)
    sub = lax.broadcasted_iota(jnp.int32, (SUB, LANES), 0)
    return lane, sub


def lanes_of(values, index):
    return jnp.take_along_axis(values, index, axis=1, mode="promise_in_bounds")


def positions(code):
    first = (code >= 3).astype(jnp.int32) + (code >= 5).astype(jnp.int32)
    second = jnp.where(code < 3, code + 1, jnp.where(code < 5, code - 1, 3))
    return first, second


def pattern_rows(pattern_ref, table, parts):
    experts = pattern_ref.shape[0]
    table[...] = jnp.zeros(table.shape, table.dtype)
    for part in range(parts):
        table[part * SUB : part * SUB + experts, :] = pattern_ref[
            :, part * LANES : (part + 1) * LANES
        ]


def row_copies(source, target, sems):
    rows = source.shape[0] // PIECES
    return [
        pltpu.make_async_copy(
            source.at[pl.ds(i * rows, rows)], target.at[pl.ds(i * rows, rows)], sems.at[i]
        )
        for i in range(PIECES)
    ]


def dispatch_kernel(
    routes_any, combine_any, scale_any, pattern_any, x_any, g_any, _a, _b, _c, *rest, n_e, holders, chunks
):
    outs, rest = rest[:2], rest[2:]
    routes, weights, scale, count, pattern, x_in, g_in, codes = rest[:8]
    x_rows, g_rows, index, stage, in_sems = rest[8:]
    moves = [
        pltpu.make_async_copy(source, target, in_sems.at[i])
        for i, (source, target) in enumerate(
            (
                (pattern_any, pattern),
                (routes_any, routes),
                (combine_any, weights),
                (scale_any, scale),
                (x_any, x_in),
                (g_any, g_in),
            )
        )
    ]
    for move in moves:
        move.start()
    experts, toks = pattern.shape[0], x_in.shape[0]
    parts = chunks // 2
    block, region = block_rows(chunks), region_rows()
    me = lax.axis_index("expert")
    lane, _ = iotas()
    stage[...] = jnp.zeros(stage.shape, F32)
    moves[0].wait()
    pattern_rows(pattern, codes, parts)
    for expert in range(experts):
        count[expert] = jnp.int32(0)
        own = codes[pl.ds(expert, SUB, stride=SUB), :]
        for odd in range(2):
            first, second = positions(lanes_of(own, lane // 2 + odd * (LANES // 2)))
            source = 4 * (lane // 2) + jnp.where(lane % 2 == 0, first, second)
            index[expert * 2 + odd] = jnp.bitwise_and(source, LANES - 1)
    for move in moves[1:]:
        move.wait()
    for ref, rows in ((x_in, x_rows), (g_in, g_rows)):
        for m in range(2 * chunks):
            rows[m * SUB : (m + 1) * SUB, :] = ref[:, m * LANES : (m + 1) * LANES].astype(F32)
        rows[2 * chunks * SUB :, :] = jnp.zeros((rows.shape[0] - 2 * chunks * SUB, LANES), F32)
    low = lane < LANES // 2
    for token in range(toks):
        for choice in range(2):
            expert = routes[choice, token]
            slot = count[expert]
            count[expert] = slot + 1
            weight = weights[choice, token] * scale[token]
            for odd in range(2):
                local = index[expert * 2 + odd]
                for array, rows in ((0, x_rows), (1, g_rows)):
                    left = rows[pl.ds(2 * odd * SUB + token, SUB, stride=4 * SUB), :]
                    right = rows[pl.ds((2 * odd + 1) * SUB + token, SUB, stride=4 * SUB), :]
                    picked = jnp.where(low, lanes_of(left, local), lanes_of(right, local))
                    if array:
                        picked = picked * weight
                    at = (expert * 2 + array) * region + slot + odd * MOST
                    stage[pl.ds(at, SUB, stride=2 * MOST), :] = picked
    for k in range(n_e):
        expert = jnp.bitwise_xor(me, k) // holders
        for array in range(2):
            at = pl.multiple_of((expert * 2 + array) * region, 16)
            to = (k // 2 * 2 + array) * block
            outs[k % 2][to : to + block, :] = stage[pl.ds(at, block), :].astype(BF16)


def region_rows():
    return -(-((SUB - 1) * 2 * MOST + 2 * MOST) // 16) * 16


def dispatch(routes, combine, scale, pattern, x, g, ws, n_e, holders, chunks):
    block, region = block_rows(chunks), region_rows()
    experts, toks = pattern.shape[0], x.shape[0]
    return pl.pallas_call(
        functools.partial(dispatch_kernel, n_e=n_e, holders=holders, chunks=chunks),
        out_shape=[vmem((n_e * block, LANES), BF16)] * 2,
        in_specs=[ANY] * 9,
        out_specs=[VMEM] * 2,
        scratch_shapes=[
            pltpu.SMEM(routes.shape, jnp.int32),
            pltpu.SMEM(combine.shape, F32),
            pltpu.SMEM(scale.shape, F32),
            pltpu.SMEM((experts,), jnp.int32),
            pltpu.VMEM(pattern.shape, jnp.int32),
            pltpu.VMEM(x.shape, BF16),
            pltpu.VMEM(g.shape, BF16),
            pltpu.VMEM((SUB * SUB, LANES), jnp.int32),
            pltpu.VMEM((4 * SUB * SUB, LANES), F32),
            pltpu.VMEM((4 * SUB * SUB, LANES), F32),
            pltpu.VMEM((experts * 2, SUB, LANES), jnp.int32),
            pltpu.VMEM((experts * 2 * region, LANES), F32),
            pltpu.SemaphoreType.DMA((6,)),
        ],
        compiler_params=params(8),
        name="dispatch",
    )(*(in_hbm(v) for v in (routes, combine, scale, pattern, x, g, *ws)))


def merge_kernel(keep, received, keep_out, send_out, *, run):
    for h in range(keep.shape[0] // run):
        at, to = slice(h * run, (h + 1) * run), h // 2 * 2 * run
        out = send_out if h % 2 else keep_out
        out[to : to + run, :] = keep[at, :]
        out[to + run : to + 2 * run, :] = received[at, :]


def merge(keep, received, run):
    return pl.pallas_call(
        functools.partial(merge_kernel, run=run),
        out_shape=[vmem(keep.shape, BF16)] * 2,
        in_specs=[VMEM] * 2,
        out_specs=[VMEM] * 2,
        compiler_params=params(8),
        name="merge",
    )(keep, received)


def exchange(keep, send, rows):
    n_e = lax.axis_size("expert")
    bit = 1
    while True:
        received = swap(send, "expert", bit)
        if 2 * bit >= n_e:
            return keep, received
        keep, send = merge(keep, received, bit * rows)
        bit *= 2


def join_kernel(blocks, out, stage, *, block, dense):
    count = blocks.shape[0] // (2 * block)
    for array in range(2):
        for k in range(count):
            at, to = (2 * k + array) * block, (array * count + k) * dense
            stage[to : to + block, :] = blocks[at : at + block, :].astype(F32)
    out[...] = stage[: 2 * count * dense, :].astype(BF16)


def join(blocks, block, dense):
    rows = blocks.shape[0] // block * dense
    return pl.pallas_call(
        functools.partial(join_kernel, block=block, dense=dense),
        out_shape=vmem((rows, LANES), BF16),
        in_specs=[VMEM],
        out_specs=VMEM,
        scratch_shapes=[pltpu.VMEM((rows + block, LANES), F32)],
        compiler_params=params(8),
        name="join",
    )(blocks)


def unpack_rows(stage, rows_ref, sources, dense, chunks):
    for c in range(chunks):
        for slot in range(MOST):
            picked = stage[pl.ds(c * MOST + slot, sources, stride=dense), :]
            rows_ref[slot * sources : (slot + 1) * sources, c * LANES : (c + 1) * LANES] = (
                picked.astype(BF16)
            )


def tile_of(size, most):
    return min(size, most)


def expert_kernel(*refs, n_t, n_e, dense, chunks):
    near, far, (wg, wu, wd), refs = refs[:n_t], refs[n_t : 2 * n_t], refs[2 * n_t :][:3], refs[2 * n_t + 3 :]
    (rows_in, rows_grad, hidden, d_gate, d_up), outs, (x_stage, g_stage) = refs[:5], refs[5:-2], refs[-2:]
    sources, size = n_e * n_t, n_e // 2 * dense
    for part, arrays in enumerate((near, far)):
        for k, ref in enumerate(arrays):
            value = ref[...].astype(F32)
            at = (2 * k + part) * size
            x_stage[at : at + size, :] = value[:size]
            g_stage[at : at + size, :] = value[size:]
    unpack_rows(x_stage, rows_in, sources, dense, chunks)
    unpack_rows(g_stage, rows_grad, sources, dense, chunks)
    last = (((1,), (1,)), ((), ()))
    hid, kept = wd.shape
    tile = tile_of(hid, 256)
    x, g = rows_in[...], rows_grad[...]
    for i in range(hid // tile):
        at = slice(i * tile, (i + 1) * tile)
        gate = jnp.dot(x, wg[:, at], preferred_element_type=F32)
        up = jnp.dot(x, wu[:, at], preferred_element_type=F32)
        grad = lax.dot_general(g, wd[at, :], last, preferred_element_type=F32)
        sig = jax.nn.sigmoid(gate)
        silu = gate * sig
        hidden[:, at] = (silu * up).astype(BF16)
        d_gate[:, at] = (grad * up * sig * (1.0 + gate * (1.0 - sig))).astype(BF16)
        d_up[:, at] = (grad * silu).astype(BF16)
    dg, du = d_gate[...], d_up[...]
    width = 2 * LANES if kept % (2 * LANES) == 0 else LANES
    for i in range(kept // width):
        at = slice(i * width, (i + 1) * width)
        back = lax.dot_general(dg, wg[at, :], last, preferred_element_type=F32)
        back = back + lax.dot_general(du, wu[at, :], last, preferred_element_type=F32)
        for half in range(width // LANES):
            c = i * (width // LANES) + half
            for slot in range(MOST):
                x_stage[pl.ds(c * MOST + slot, sources, stride=dense), :] = back[
                    slot * sources : (slot + 1) * sources, half * LANES : (half + 1) * LANES
                ]
    for k in range(n_t):
        outs[k][...] = x_stage[2 * k * size : 2 * (k + 1) * size, :].astype(BF16)


def expert_rows(near, far, wg, wu, wd, n_e, dense, chunks):
    n_t = len(near)
    count = MOST * n_e * n_t
    kept, hid = wg.shape
    return pl.pallas_call(
        functools.partial(expert_kernel, n_t=n_t, n_e=n_e, dense=dense, chunks=chunks),
        out_shape=[vmem((count, kept), BF16)] * 2
        + [vmem((count, hid), BF16)] * 3
        + [vmem((n_e * dense, LANES), BF16)] * n_t,
        in_specs=[VMEM] * (2 * n_t + 3),
        out_specs=[VMEM] * (5 + n_t),
        scratch_shapes=[pltpu.VMEM((n_t * n_e * dense, LANES), F32)] * 2,
        compiler_params=params(20),
        cost_estimate=cost(10 * 4 * count * kept * hid, 6 * kept * hid),
        name="expert_rows",
    )(*near, *far, wg, wu, wd)


def outer_kernel(left, *refs, count, tile, width):
    rights, outs, token = refs[:count], refs[count : 2 * count], refs[2 * count]
    held, sems = refs[2 * count + 1 :]
    first = (((0,), (0,)), ((), ()))
    token[...] = jnp.zeros(TOKEN, F32)
    m, n = outs[0].shape
    moves = []
    for i in range(m // tile):
        rows = pl.ds(i * tile, tile)
        for array in range(count):
            for j in range(n // width):
                at = slice(j * width, (j + 1) * width)
                value = lax.dot_general(
                    left[:, i * tile : (i + 1) * tile],
                    rights[array][:, at],
                    first,
                    preferred_element_type=F32,
                )
                held[array, rows, at] = value.astype(BF16)
            move = pltpu.make_async_copy(
                held.at[array, rows], outs[array].at[rows], sems.at[array, i]
            )
            move.start()
            moves.append(move)
    for move in moves:
        move.wait()


def outer(left, rights, name):
    rows, m = left.shape
    n = rights[0].shape[1]
    count = len(rights)
    tile, width = tile_of(m, 256), tile_of(n, 512)
    return pl.pallas_call(
        functools.partial(outer_kernel, count=count, tile=tile, width=width),
        out_shape=[jax.ShapeDtypeStruct((m, n), BF16)] * count + [vmem(TOKEN, F32)],
        in_specs=[VMEM] * (1 + count),
        out_specs=[ANY] * count + [VMEM],
        scratch_shapes=[
            pltpu.VMEM((count, m, n), BF16),
            pltpu.SemaphoreType.DMA((count, m // tile)),
        ],
        compiler_params=params(28),
        cost_estimate=cost(2 * 256 * m * n * count, 2 * m * n * count),
        name=name,
    )(left, *rights)


def sum_kernel(*refs, n_t, n_e, block, dense):
    ins, (token, keep, send, stage) = refs[:n_t], refs[n_t:]
    total = ins[0][...].astype(F32)
    for ref in ins[1:]:
        total = total + ref[...].astype(F32)
    stage[: n_e * dense, :] = total
    stage[n_e * dense :, :] = jnp.zeros((stage.shape[0] - n_e * dense, LANES), F32)
    for k in range(n_e):
        out = send if k % 2 else keep
        value = stage[k * dense : k * dense + block, :].astype(BF16)
        out[k // 2 * block : (k // 2 + 1) * block, :] = value


def sum_parts(arrays, token, n_e, block, dense):
    n_t = len(arrays)
    return pl.pallas_call(
        functools.partial(sum_kernel, n_t=n_t, n_e=n_e, block=block, dense=dense),
        out_shape=[vmem((n_e // 2 * block, LANES), BF16)] * 2,
        in_specs=[VMEM] * (n_t + 1),
        out_specs=[VMEM] * 2,
        scratch_shapes=[pltpu.VMEM((n_e * dense + block, LANES), F32)],
        compiler_params=params(8),
        name="sum_parts",
    )(*arrays, token)


def combine_kernel(routes, pattern, *rest, n_e, holders, chunks):
    ins, (out, count, codes, index, stage, spread) = rest[:2], rest[2:]
    experts, toks = pattern.shape[0], out.shape[0]
    block = 2 * ins[0].shape[0] // n_e
    me = lax.axis_index("expert")
    lane, _ = iotas()
    for half, ref in enumerate(ins):
        rows = ref.shape[0]
        stage[half * rows : (half + 1) * rows, :] = ref[...].astype(F32)
    tail = stage.shape[0] - n_e * block
    stage[n_e * block :, :] = jnp.zeros((tail, LANES), F32)
    pattern_rows(pattern, codes, chunks // 2)
    for expert in range(experts):
        count[expert] = jnp.int32(0)
        own = codes[pl.ds(expert, SUB, stride=SUB), :]
        for quarter in range(4):
            first, second = positions(lanes_of(own, lane // 4 + quarter * (LANES // 4)))
            place = lane % 4
            later = place == second
            local = (quarter % 2) * (LANES // 2) + 2 * (lane // 4) + later.astype(jnp.int32)
            keep = jnp.logical_or(place == first, later)
            index[expert * 4 + quarter] = jnp.where(keep, local, -1)
    for token in range(toks):
        total = [None] * 4
        for choice in range(2):
            expert = routes[choice, token]
            slot = count[expert]
            count[expert] = slot + 1
            for odd in range(2):
                row = None
                for holder in range(holders):
                    k = jnp.bitwise_xor(me, expert * holders + holder)
                    part = stage[pl.ds(k * block + slot + odd * MOST, SUB, stride=2 * MOST), :]
                    row = part if row is None else row + part
                for half in range(2):
                    quarter = 2 * odd + half
                    local = index[expert * 4 + quarter]
                    value = lanes_of(row, jnp.bitwise_and(local, LANES - 1))
                    value = jnp.where(local >= 0, value, 0.0)
                    total[quarter] = value if choice == 0 else total[quarter] + value
        for quarter in range(4):
            spread[pl.ds(quarter * SUB + token, SUB, stride=4 * SUB), :] = total[quarter]
    for m in range(2 * chunks):
        out[:, m * LANES : (m + 1) * LANES] = spread[m * SUB : (m + 1) * SUB, :].astype(BF16)


def combine_rows(routes, pattern, arrays, toks, width, n_e, holders, chunks):
    block = 2 * arrays[0].shape[0] // n_e
    experts = pattern.shape[0]
    return pl.pallas_call(
        functools.partial(combine_kernel, n_e=n_e, holders=holders, chunks=chunks),
        out_shape=jax.ShapeDtypeStruct((toks, width), BF16),
        in_specs=[SMEM, VMEM] + [VMEM] * 2,
        out_specs=VMEM,
        scratch_shapes=[
            pltpu.SMEM((experts,), jnp.int32),
            pltpu.VMEM((SUB * SUB, LANES), jnp.int32),
            pltpu.VMEM((experts * 4, SUB, LANES), jnp.int32),
            pltpu.VMEM((n_e * block + region_rows() - block, LANES), F32),
            pltpu.VMEM((4 * SUB * SUB, LANES), F32),
        ],
        compiler_params=params(8),
        name="combine_rows",
    )(routes, pattern, *arrays)


def swap(value, axis, k):
    size = lax.axis_size(axis)
    return lax.ppermute(value, axis, [(i, i ^ k) for i in range(size)])


def cross(value, mask):
    size = lax.axis_size("expert") * lax.axis_size("tensor")
    return lax.ppermute(value, ("expert", "tensor"), [(i, i ^ mask) for i in range(size)])


def gather_line(value, across):
    far = lax.axis_size("tensor") // 2
    start = across * lax.axis_size("tensor")
    held = {0: cross(value, start) if across else value}
    if far:
        held[far] = cross(value, start + far)
    bit = far // 2
    while bit:
        for k in list(held):
            held[k ^ bit] = cross(held[k], bit)
        bit //= 2
    return [held[k] for k in range(len(held))]


def body(x_tokens, grad_values, grad_scale, combine, routes, pattern, w_gate, w_up, w_down):
    n_e = lax.axis_size("expert")
    n_t = lax.axis_size("tensor")
    experts = pattern.shape[0]
    holders = n_e // experts
    toks, width = x_tokens.shape
    chunks = w_gate.shape[0] // LANES
    block = block_rows(chunks)
    dense = chunks * MOST

    routes, combine = routes.T, combine.T
    keep, send = dispatch(
        routes, combine, grad_scale, pattern, x_tokens, grad_values, (w_gate, w_up, w_down), n_e, holders, chunks
    )
    bit = 1
    while 2 * bit < n_e:
        keep, send = merge(keep, swap(send, "expert", bit), bit * 2 * block)
        bit *= 2
    near = gather_line(join(keep, block, dense), 0)
    far = gather_line(join(send, block, dense), bit)
    rows_in, rows_grad, hidden, d_gate, d_up, *back = expert_rows(
        near, far, w_gate, w_up, w_down, n_e, dense, chunks
    )
    back = [back[0]] + [swap(back[k], "tensor", k) for k in range(1, n_t)]
    part_gate, part_up, token = outer(rows_in, [d_gate, d_up], "grads_in")
    keep, send = sum_parts(back, token, n_e, block, dense)
    summed = exchange(keep, send, block)
    part_down, _ = outer(hidden, [rows_grad], "grad_down")
    grad_tokens = combine_rows(routes, pattern, summed, toks, width, n_e, holders, chunks)
    return grad_tokens, part_gate, part_up, part_down


def solution(mesh):
    in_specs = (
        P(("group", "expert", "tensor"), None),
        P(("group", "expert", "tensor"), None),
        P(("group", "expert", "tensor")),
        P(("group", "expert", "tensor"), None),
        P(("group", "expert", "tensor"), None),
        P(),
        P(None, ("expert", "tensor")),
        P(None, ("expert", "tensor")),
        P(("expert", "tensor"), None),
    )
    out_specs = (
        P(("group", "expert", "tensor"), None),
        P("group", ("expert", "tensor")),
        P("group", ("expert", "tensor")),
        P(("expert", "tensor"), "group"),
    )
    return jax.shard_map(body, mesh=mesh, in_specs=in_specs, out_specs=out_specs, check_vma=False)
```

```python
import functools

import jax
import jax.numpy as jnp
from jax import lax
from jax.experimental import pallas as pl
from jax.experimental.pallas import tpu as pltpu
from jax.sharding import PartitionSpec as P

MOST = 5
LANES = 128
SUB = 8
PIECES = 4
TOKEN = (SUB, LANES)
F32 = jnp.float32
BF16 = jnp.bfloat16
VMEM = pl.BlockSpec(memory_space=pltpu.VMEM)
SMEM = pl.BlockSpec(memory_space=pltpu.SMEM)
ANY = pl.BlockSpec(memory_space=pl.ANY)


def vmem(shape, dtype):
    return pltpu.VMEM(shape, dtype)


def in_hbm(value):
    return pltpu.with_memory_space_constraint(value, pltpu.HBM)


def params(mib=48):
    return pltpu.CompilerParams(vmem_limit_bytes=mib << 20)


def cost(flops, bytes_accessed):
    return pl.CostEstimate(flops=int(flops), bytes_accessed=int(bytes_accessed), transcendentals=0)


def block_rows(chunks):
    return -(-((chunks - 1) * MOST + SUB) // 16) * 16


def iotas():
    lane = lax.broadcasted_iota(jnp.int32, (SUB, LANES), 1)
    sub = lax.broadcasted_iota(jnp.int32, (SUB, LANES), 0)
    return lane, sub


def lanes_of(values, index):
    return jnp.take_along_axis(values, index, axis=1, mode="promise_in_bounds")


def positions(code):
    first = (code >= 3).astype(jnp.int32) + (code >= 5).astype(jnp.int32)
    second = jnp.where(code < 3, code + 1, jnp.where(code < 5, code - 1, 3))
    return first, second


def pattern_rows(pattern_ref, table, parts):
    experts = pattern_ref.shape[0]
    table[...] = jnp.zeros(table.shape, table.dtype)
    for part in range(parts):
        table[part * SUB : part * SUB + experts, :] = pattern_ref[
            :, part * LANES : (part + 1) * LANES
        ]


def row_copies(source, target, sems):
    rows = source.shape[0] // PIECES
    return [
        pltpu.make_async_copy(
            source.at[pl.ds(i * rows, rows)], target.at[pl.ds(i * rows, rows)], sems.at[i]
        )
        for i in range(PIECES)
    ]


def dispatch_kernel(
    routes_any, combine_any, scale_any, pattern_any, x_any, g_any, _a, _b, _c, *rest, n_e, holders, chunks
):
    outs, rest = rest[:2], rest[2:]
    routes, weights, scale, count, pattern, x_in, g_in, codes = rest[:8]
    x_rows, g_rows, index, stage, in_sems = rest[8:]
    moves = [
        pltpu.make_async_copy(source, target, in_sems.at[i])
        for i, (source, target) in enumerate(
            (
                (pattern_any, pattern),
                (routes_any, routes),
                (combine_any, weights),
                (scale_any, scale),
                (x_any, x_in),
                (g_any, g_in),
            )
        )
    ]
    for move in moves:
        move.start()
    experts, toks = pattern.shape[0], x_in.shape[0]
    parts = chunks // 2
    block, region = block_rows(chunks), region_rows()
    me = lax.axis_index("expert")
    lane, _ = iotas()
    stage[...] = jnp.zeros(stage.shape, F32)
    moves[0].wait()
    pattern_rows(pattern, codes, parts)
    for expert in range(experts):
        count[expert] = jnp.int32(0)
        own = codes[pl.ds(expert, SUB, stride=SUB), :]
        for odd in range(2):
            first, second = positions(lanes_of(own, lane // 2 + odd * (LANES // 2)))
            source = 4 * (lane // 2) + jnp.where(lane % 2 == 0, first, second)
            index[expert * 2 + odd] = jnp.bitwise_and(source, LANES - 1)
    for move in moves[1:]:
        move.wait()
    for ref, rows in ((x_in, x_rows), (g_in, g_rows)):
        for m in range(2 * chunks):
            rows[m * SUB : (m + 1) * SUB, :] = ref[:, m * LANES : (m + 1) * LANES].astype(F32)
        rows[2 * chunks * SUB :, :] = jnp.zeros((rows.shape[0] - 2 * chunks * SUB, LANES), F32)
    low = lane < LANES // 2
    for token in range(toks):
        for choice in range(2):
            expert = routes[choice, token]
            slot = count[expert]
            count[expert] = slot + 1
            weight = weights[choice, token] * scale[token]
            for odd in range(2):
                local = index[expert * 2 + odd]
                for array, rows in ((0, x_rows), (1, g_rows)):
                    left = rows[pl.ds(2 * odd * SUB + token, SUB, stride=4 * SUB), :]
                    right = rows[pl.ds((2 * odd + 1) * SUB + token, SUB, stride=4 * SUB), :]
                    picked = jnp.where(low, lanes_of(left, local), lanes_of(right, local))
                    if array:
                        picked = picked * weight
                    at = (expert * 2 + array) * region + slot + odd * MOST
                    stage[pl.ds(at, SUB, stride=2 * MOST), :] = picked
    for k in range(n_e):
        expert = jnp.bitwise_xor(me, k) // holders
        for array in range(2):
            at = pl.multiple_of((expert * 2 + array) * region, 16)
            to = (k // 2 * 2 + array) * block
            outs[k % 2][to : to + block, :] = stage[pl.ds(at, block), :].astype(BF16)


def region_rows():
    return -(-((SUB - 1) * 2 * MOST + 2 * MOST) // 16) * 16


def dispatch(routes, combine, scale, pattern, x, g, ws, n_e, holders, chunks):
    block, region = block_rows(chunks), region_rows()
    experts, toks = pattern.shape[0], x.shape[0]
    return pl.pallas_call(
        functools.partial(dispatch_kernel, n_e=n_e, holders=holders, chunks=chunks),
        out_shape=[vmem((n_e * block, LANES), BF16)] * 2,
        in_specs=[ANY] * 9,
        out_specs=[VMEM] * 2,
        scratch_shapes=[
            pltpu.SMEM(routes.shape, jnp.int32),
            pltpu.SMEM(combine.shape, F32),
            pltpu.SMEM(scale.shape, F32),
            pltpu.SMEM((experts,), jnp.int32),
            pltpu.VMEM(pattern.shape, jnp.int32),
            pltpu.VMEM(x.shape, BF16),
            pltpu.VMEM(g.shape, BF16),
            pltpu.VMEM((SUB * SUB, LANES), jnp.int32),
            pltpu.VMEM((4 * SUB * SUB, LANES), F32),
            pltpu.VMEM((4 * SUB * SUB, LANES), F32),
            pltpu.VMEM((experts * 2, SUB, LANES), jnp.int32),
            pltpu.VMEM((experts * 2 * region, LANES), F32),
            pltpu.SemaphoreType.DMA((6,)),
        ],
        compiler_params=params(8),
        name="dispatch",
    )(*(in_hbm(v) for v in (routes, combine, scale, pattern, x, g, *ws)))


def merge_kernel(keep, received, keep_out, send_out, *, run):
    for h in range(keep.shape[0] // run):
        at, to = slice(h * run, (h + 1) * run), h // 2 * 2 * run
        out = send_out if h % 2 else keep_out
        out[to : to + run, :] = keep[at, :]
        out[to + run : to + 2 * run, :] = received[at, :]


def merge(keep, received, run):
    return pl.pallas_call(
        functools.partial(merge_kernel, run=run),
        out_shape=[vmem(keep.shape, BF16)] * 2,
        in_specs=[VMEM] * 2,
        out_specs=[VMEM] * 2,
        compiler_params=params(8),
        name="merge",
    )(keep, received)


def exchange(keep, send, rows):
    n_e = lax.axis_size("expert")
    bit = 1
    while True:
        received = swap(send, "expert", bit)
        if 2 * bit >= n_e:
            return keep, received
        keep, send = merge(keep, received, bit * rows)
        bit *= 2


def join_kernel(blocks, out, stage, *, block, dense):
    count = blocks.shape[0] // (2 * block)
    for array in range(2):
        for k in range(count):
            at, to = (2 * k + array) * block, (array * count + k) * dense
            stage[to : to + block, :] = blocks[at : at + block, :].astype(F32)
    out[...] = stage[: 2 * count * dense, :].astype(BF16)


def join(blocks, block, dense):
    rows = blocks.shape[0] // block * dense
    return pl.pallas_call(
        functools.partial(join_kernel, block=block, dense=dense),
        out_shape=vmem((rows, LANES), BF16),
        in_specs=[VMEM],
        out_specs=VMEM,
        scratch_shapes=[pltpu.VMEM((rows + block, LANES), F32)],
        compiler_params=params(8),
        name="join",
    )(blocks)


def unpack_rows(stage, rows_ref, sources, dense, chunks):
    for c in range(chunks):
        for slot in range(MOST):
            picked = stage[pl.ds(c * MOST + slot, sources, stride=dense), :]
            rows_ref[slot * sources : (slot + 1) * sources, c * LANES : (c + 1) * LANES] = (
                picked.astype(BF16)
            )


def tile_of(size, most):
    return min(size, most)


def expert_kernel(*refs, n_t, n_e, dense, chunks):
    near, far, (wg, wu, wd), refs = refs[:n_t], refs[n_t : 2 * n_t], refs[2 * n_t :][:3], refs[2 * n_t + 3 :]
    (rows_in, rows_grad, hidden, d_gate, d_up), outs, (x_stage, g_stage) = refs[:5], refs[5:-2], refs[-2:]
    sources, size = n_e * n_t, n_e // 2 * dense
    for part, arrays in enumerate((near, far)):
        for k, ref in enumerate(arrays):
            value = ref[...].astype(F32)
            at = (2 * k + part) * size
            x_stage[at : at + size, :] = value[:size]
            g_stage[at : at + size, :] = value[size:]
    unpack_rows(x_stage, rows_in, sources, dense, chunks)
    unpack_rows(g_stage, rows_grad, sources, dense, chunks)
    last = (((1,), (1,)), ((), ()))
    hid, kept = wd.shape
    tile = tile_of(hid, 256)
    x, g = rows_in[...], rows_grad[...]
    for i in range(hid // tile):
        at = slice(i * tile, (i + 1) * tile)
        gate = jnp.dot(x, wg[:, at], preferred_element_type=F32)
        up = jnp.dot(x, wu[:, at], preferred_element_type=F32)
        grad = lax.dot_general(g, wd[at, :], last, preferred_element_type=F32)
        sig = jax.nn.sigmoid(gate)
        silu = gate * sig
        hidden[:, at] = (silu * up).astype(BF16)
        d_gate[:, at] = (grad * up * sig * (1.0 + gate * (1.0 - sig))).astype(BF16)
        d_up[:, at] = (grad * silu).astype(BF16)
    dg, du = d_gate[...], d_up[...]
    width = 2 * LANES if kept % (2 * LANES) == 0 else LANES
    for i in range(kept // width):
        at = slice(i * width, (i + 1) * width)
        back = lax.dot_general(dg, wg[at, :], last, preferred_element_type=F32)
        back = back + lax.dot_general(du, wu[at, :], last, preferred_element_type=F32)
        for half in range(width // LANES):
            c = i * (width // LANES) + half
            for slot in range(MOST):
                x_stage[pl.ds(c * MOST + slot, sources, stride=dense), :] = back[
                    slot * sources : (slot + 1) * sources, half * LANES : (half + 1) * LANES
                ]
    for k in range(n_t):
        outs[k][...] = x_stage[2 * k * size : 2 * (k + 1) * size, :].astype(BF16)


def expert_rows(near, far, wg, wu, wd, n_e, dense, chunks):
    n_t = len(near)
    count = MOST * n_e * n_t
    kept, hid = wg.shape
    return pl.pallas_call(
        functools.partial(expert_kernel, n_t=n_t, n_e=n_e, dense=dense, chunks=chunks),
        out_shape=[vmem((count, kept), BF16)] * 2
        + [vmem((count, hid), BF16)] * 3
        + [vmem((n_e * dense, LANES), BF16)] * n_t,
        in_specs=[VMEM] * (2 * n_t + 3),
        out_specs=[VMEM] * (5 + n_t),
        scratch_shapes=[pltpu.VMEM((n_t * n_e * dense, LANES), F32)] * 2,
        compiler_params=params(20),
        cost_estimate=cost(10 * 4 * count * kept * hid, 6 * kept * hid),
        name="expert_rows",
    )(*near, *far, wg, wu, wd)


def outer_kernel(left, *refs, count, tile, width):
    rights, outs, token = refs[:count], refs[count : 2 * count], refs[2 * count]
    held, sems = refs[2 * count + 1 :]
    first = (((0,), (0,)), ((), ()))
    token[...] = jnp.zeros(TOKEN, F32)
    m, n = outs[0].shape
    moves = []
    for i in range(m // tile):
        rows = pl.ds(i * tile, tile)
        for array in range(count):
            for j in range(n // width):
                at = slice(j * width, (j + 1) * width)
                value = lax.dot_general(
                    left[:, i * tile : (i + 1) * tile],
                    rights[array][:, at],
                    first,
                    preferred_element_type=F32,
                )
                held[array, rows, at] = value.astype(BF16)
            move = pltpu.make_async_copy(
                held.at[array, rows], outs[array].at[rows], sems.at[array, i]
            )
            move.start()
            moves.append(move)
    for move in moves:
        move.wait()


def outer(left, rights, name):
    rows, m = left.shape
    n = rights[0].shape[1]
    count = len(rights)
    tile, width = tile_of(m, 256), tile_of(n, 512)
    return pl.pallas_call(
        functools.partial(outer_kernel, count=count, tile=tile, width=width),
        out_shape=[jax.ShapeDtypeStruct((m, n), BF16)] * count + [vmem(TOKEN, F32)],
        in_specs=[VMEM] * (1 + count),
        out_specs=[ANY] * count + [VMEM],
        scratch_shapes=[
            pltpu.VMEM((count, m, n), BF16),
            pltpu.SemaphoreType.DMA((count, m // tile)),
        ],
        compiler_params=params(28),
        cost_estimate=cost(2 * 256 * m * n * count, 2 * m * n * count),
        name=name,
    )(left, *rights)


def sum_kernel(*refs, n_t, n_e, block, dense):
    ins, (token, keep, send, stage) = refs[:n_t], refs[n_t:]
    total = ins[0][...].astype(F32)
    for ref in ins[1:]:
        total = total + ref[...].astype(F32)
    stage[: n_e * dense, :] = total
    stage[n_e * dense :, :] = jnp.zeros((stage.shape[0] - n_e * dense, LANES), F32)
    for k in range(n_e):
        out = send if k % 2 else keep
        value = stage[k * dense : k * dense + block, :].astype(BF16)
        out[k // 2 * block : (k // 2 + 1) * block, :] = value


def sum_parts(arrays, token, n_e, block, dense):
    n_t = len(arrays)
    return pl.pallas_call(
        functools.partial(sum_kernel, n_t=n_t, n_e=n_e, block=block, dense=dense),
        out_shape=[vmem((n_e // 2 * block, LANES), BF16)] * 2,
        in_specs=[VMEM] * (n_t + 1),
        out_specs=[VMEM] * 2,
        scratch_shapes=[pltpu.VMEM((n_e * dense + block, LANES), F32)],
        compiler_params=params(8),
        name="sum_parts",
    )(*arrays, token)


def combine_kernel(routes, pattern, *rest, n_e, holders, chunks):
    ins, (out, count, codes, index, stage, spread) = rest[:2], rest[2:]
    experts, toks = pattern.shape[0], out.shape[0]
    block = 2 * ins[0].shape[0] // n_e
    me = lax.axis_index("expert")
    lane, _ = iotas()
    for half, ref in enumerate(ins):
        rows = ref.shape[0]
        stage[half * rows : (half + 1) * rows, :] = ref[...].astype(F32)
    tail = stage.shape[0] - n_e * block
    stage[n_e * block :, :] = jnp.zeros((tail, LANES), F32)
    pattern_rows(pattern, codes, chunks // 2)
    for expert in range(experts):
        count[expert] = jnp.int32(0)
        own = codes[pl.ds(expert, SUB, stride=SUB), :]
        for quarter in range(4):
            first, second = positions(lanes_of(own, lane // 4 + quarter * (LANES // 4)))
            place = lane % 4
            later = place == second
            local = (quarter % 2) * (LANES // 2) + 2 * (lane // 4) + later.astype(jnp.int32)
            keep = jnp.logical_or(place == first, later)
            index[expert * 4 + quarter] = jnp.where(keep, local, -1)
    for token in range(toks):
        total = [None] * 4
        for choice in range(2):
            expert = routes[choice, token]
            slot = count[expert]
            count[expert] = slot + 1
            for odd in range(2):
                row = None
                for holder in range(holders):
                    k = jnp.bitwise_xor(me, expert * holders + holder)
                    part = stage[pl.ds(k * block + slot + odd * MOST, SUB, stride=2 * MOST), :]
                    row = part if row is None else row + part
                for half in range(2):
                    quarter = 2 * odd + half
                    local = index[expert * 4 + quarter]
                    value = lanes_of(row, jnp.bitwise_and(local, LANES - 1))
                    value = jnp.where(local >= 0, value, 0.0)
                    total[quarter] = value if choice == 0 else total[quarter] + value
        for quarter in range(4):
            spread[pl.ds(quarter * SUB + token, SUB, stride=4 * SUB), :] = total[quarter]
    for m in range(2 * chunks):
        out[:, m * LANES : (m + 1) * LANES] = spread[m * SUB : (m + 1) * SUB, :].astype(BF16)


def combine_rows(routes, pattern, arrays, toks, width, n_e, holders, chunks):
    block = 2 * arrays[0].shape[0] // n_e
    experts = pattern.shape[0]
    return pl.pallas_call(
        functools.partial(combine_kernel, n_e=n_e, holders=holders, chunks=chunks),
        out_shape=jax.ShapeDtypeStruct((toks, width), BF16),
        in_specs=[SMEM, VMEM] + [VMEM] * 2,
        out_specs=VMEM,
        scratch_shapes=[
            pltpu.SMEM((experts,), jnp.int32),
            pltpu.VMEM((SUB * SUB, LANES), jnp.int32),
            pltpu.VMEM((experts * 4, SUB, LANES), jnp.int32),
            pltpu.VMEM((n_e * block + region_rows() - block, LANES), F32),
            pltpu.VMEM((4 * SUB * SUB, LANES), F32),
        ],
        compiler_params=params(8),
        name="combine_rows",
    )(routes, pattern, *arrays)


def swap(value, axis, k):
    size = lax.axis_size(axis)
    return lax.ppermute(value, axis, [(i, i ^ k) for i in range(size)])


def cross(value, mask):
    size = lax.axis_size("expert") * lax.axis_size("tensor")
    return lax.ppermute(value, ("expert", "tensor"), [(i, i ^ mask) for i in range(size)])


def gather_line(value, across):
    n_t = lax.axis_size("tensor")
    start = across * n_t
    held = {0: cross(value, start) if across else value}
    for k in range(1, n_t):
        rest = k & (k - 1)
        held[k] = cross(held[rest], k - rest) if rest else cross(value, start + k)
    return [held[k] for k in range(n_t)]


def body(x_tokens, grad_values, grad_scale, combine, routes, pattern, w_gate, w_up, w_down):
    n_e = lax.axis_size("expert")
    n_t = lax.axis_size("tensor")
    experts = pattern.shape[0]
    holders = n_e // experts
    toks, width = x_tokens.shape
    chunks = w_gate.shape[0] // LANES
    block = block_rows(chunks)
    dense = chunks * MOST

    routes, combine = routes.T, combine.T
    keep, send = dispatch(
        routes, combine, grad_scale, pattern, x_tokens, grad_values, (w_gate, w_up, w_down), n_e, holders, chunks
    )
    bit = 1
    while 2 * bit < n_e:
        keep, send = merge(keep, swap(send, "expert", bit), bit * 2 * block)
        bit *= 2
    near = gather_line(join(keep, block, dense), 0)
    far = gather_line(join(send, block, dense), bit)
    rows_in, rows_grad, hidden, d_gate, d_up, *back = expert_rows(
        near, far, w_gate, w_up, w_down, n_e, dense, chunks
    )
    back = [back[0]] + [swap(back[k], "tensor", k) for k in range(1, n_t)]
    part_gate, part_up, token = outer(rows_in, [d_gate, d_up], "grads_in")
    keep, send = sum_parts(back, token, n_e, block, dense)
    summed = exchange(keep, send, block)
    part_down, _ = outer(hidden, [rows_grad], "grad_down")
    grad_tokens = combine_rows(routes, pattern, summed, toks, width, n_e, holders, chunks)
    return grad_tokens, part_gate, part_up, part_down


def solution(mesh):
    in_specs = (
        P(("group", "expert", "tensor"), None),
        P(("group", "expert", "tensor"), None),
        P(("group", "expert", "tensor")),
        P(("group", "expert", "tensor"), None),
        P(("group", "expert", "tensor"), None),
        P(),
        P(None, ("expert", "tensor")),
        P(None, ("expert", "tensor")),
        P(("expert", "tensor"), None),
    )
    out_specs = (
        P(("group", "expert", "tensor"), None),
        P("group", ("expert", "tensor")),
        P("group", ("expert", "tensor")),
        P(("expert", "tensor"), "group"),
    )
    return jax.shard_map(body, mesh=mesh, in_specs=in_specs, out_specs=out_specs, check_vma=False)
```
